256 devices in a mesh: dp: 8 (over x, core), expert: 32 (over z, y).
Axes of the slice: x: 4, y: 4, z: 8, core: 2. Of those that a mesh axis runs over, the one named last changes fastest.
Arguments:
- tokens: bfloat16 [32768, 2048], P(('dp', 'expert')), may hold values from -6 to 6
- expert_ids: int32 [32768, 8], P('dp'), may hold values from 0 to 31, all different within a row; in each aligned block of 128 rows (0 to 127, 128 to 255, ...) at most 48 rows name the same one
- gate_weights: float32 [32768, 8], P(('dp', 'expert')), may hold values from 0.25 to 2
- span_ids: int32 [8, 4096], P(None, 'expert'), may hold values from 0 to 63, as said below
- w_gate: bfloat16 [32, 2048, 768], P('expert'), may hold values from -0.125 to 0.125
- w_up: bfloat16 [32, 2048, 768], P('expert'), may hold values from -0.125 to 0.125
- w_down: bfloat16 [32, 768, 2048], P('expert'), may hold values from -0.21875 to 0.21875
- w_proj: bfloat16 [2048, 2560], P(None, 'dp'), may hold values from -0.125 to 0.125
- cotangent: bfloat16 [8, 2048, 2560], P(None, 'expert', 'dp'), may hold values from -0.046875 to 0.046875
Outputs:
- student: bfloat16 [8, 2048, 2560], P(None, 'expert', 'dp')
- grad_proj: float32 [2048, 2560], P('expert', 'dp')
The draws below stay inside these ranges and needn't reach their ends.
Inputs may be any that keep to these rules, and one draw needn't show every extreme that they name: `expert_ids`: each row names 8 different experts. Within each aligned block of 128 rows (the tokens of one device) no expert is named by more than 48 rows, and in some blocks one expert is named by exactly 48. `span_ids`: each run of 128 entries of a row (one device's tokens) holds the span numbers 0 to 63 in order, never falling; each span has 1 to 4 tokens, and exactly one span of each run has 4.
All inputs are finite; a program needn't handle non-finite values.
Results may differ from the reference program's by a relative error of at most 0.015.
Values may be sent and summed in bfloat16 or wider, within the bound.
A program may use at most 128 MiB of HBM per device.

```python
import math
import jax
import jax.numpy as jnp
import numpy as np
from jax import lax

D = 2048
FF = 768
TOPK = 8
SD = 2560
TOK_DEV = 128
EXPERTS = 32
CAP = 48
SPANS_DEV = 64
SPANS_GRP = 2048
TOKENS = 32768
SPANS = 16384
N_DP = 8
N_EXPERT = 32


def draw_span_ids(key, part):
    key = jax.random.fold_in(key, 7)
    first, second, third = jax.random.split(key, 3)
    blocks = N_DP * N_EXPERT
    pairs = TOK_DEV // 4
    delta = jax.random.randint(first, (blocks, pairs), -1, 2)
    lengths = jnp.stack([2 + delta, 2 - delta], axis=-1).reshape(blocks, 2 * pairs)
    quads = TOK_DEV // 8
    chosen = jax.random.randint(second, (blocks, 1), 0, quads)
    turn = jax.random.randint(third, (blocks, 1), 0, 4)
    index = jnp.arange(2 * pairs, dtype=jnp.int32)[None, :]
    within = (index + turn) % 4
    pattern = jnp.where(within == 0, 4, jnp.where(within == 3, 2, 1))
    lengths = jnp.where(index // 4 == chosen, pattern, lengths).astype(jnp.int32)
    ends = jnp.cumsum(lengths, axis=1)
    position = jnp.arange(TOK_DEV, dtype=jnp.int32)
    spans = jnp.sum((ends[:, None, :] <= position[None, :, None]).astype(jnp.int32), axis=-1)
    return spans.reshape(N_DP, N_EXPERT * TOK_DEV).astype(jnp.int32)


def block_levels(own_key, shape, cuts, smallest, high):
    gain = 1.0
    for dim, blocks in cuts:
        draws = jax.random.uniform(jax.random.fold_in(jax.random.fold_in(own_key, 6), dim), (blocks,), jnp.float32, smallest / len(cuts), high / len(cuts))
        gain = gain * jnp.repeat(jnp.exp(draws), shape[dim] // blocks).reshape((-1,) + (1,) * (len(shape) - 1 - dim))
    return gain


def deal_out(rng, own, number, rows, amount, top, most, skew):
    ranking = jax.random.permutation(rng, amount)
    packed, common = load_shares(amount, rows * top, most, skew, True), load_shares(amount, rows * top, most, skew, False)
    places = jnp.arange(amount)

    def named(tallies, offset_by):
        used = int((tallies > 0).sum())
        fixed = max(1, used // 4)
        passed = fixed + (places - fixed + offset_by * (used - fixed)) % max(1, amount - fixed)
        return jnp.zeros((amount,), jnp.int32).at[ranking[jnp.where(places < fixed, places, passed)]].set(jnp.asarray(tallies, jnp.int32))

    tallies = jnp.where(number % 4 == 0, named(packed, number // 4), named(common, number - number // 4 - 1))
    mixed = jax.random.permutation(jax.random.fold_in(own, 3), amount)
    giver, taker = mixed[0:amount // 2 * 2:2], mixed[1:amount // 2 * 2:2]
    margin = jnp.minimum(tallies[giver] - 1, most - tallies[taker]) // 2
    margin = jnp.where((giver == ranking[0]) | (taker == ranking[0]) | (tallies[taker] == 0), 0, jnp.maximum(margin, 0))
    passed = jax.random.randint(jax.random.fold_in(own, 4), (amount // 2,), 0, 1 << 20) % (margin + 1)
    tallies = tallies.at[giver].add(-passed).at[taker].add(passed)
    items = jnp.searchsorted(jnp.cumsum(tallies), jnp.arange(rows * top), side="right").astype(jnp.int32)
    table = items.reshape(top, rows).T
    table = table[jax.random.permutation(jax.random.fold_in(own, 1), rows)]
    offset_by = jax.random.randint(jax.random.fold_in(own, 2), (rows, 1), 0, top)
    return jnp.take_along_axis(table, (jnp.arange(top)[None, :] + offset_by) % top, axis=1)


def load_shares(count, total, reach, slope, full):
    portions = [(1 << 20) // math.isqrt(rank ** slope) + 1 for rank in range(1, count + 1)]
    largest = reach if full else min(reach, max(-(-total // count), total * portions[0] // sum(portions)))
    least = 1 if total - largest >= count - 1 else 0
    given, surplus = [largest] + [least] * (count - 1), total - largest - least * (count - 1)
    while surplus > 0:
        free = [i for i in range(1, count) if given[i] < largest] or [i for i in range(1, count) if given[i] < reach]
        pool, left = sum([portions[i] for i in free]), surplus
        for i in free:
            more = min(reach - given[i], max(1, left * portions[i] // pool), surplus)
            given[i] = given[i] + more
            surplus = surplus - more
    return np.array(given)


def scatter_about(rng, extent, width, most, pieces=(), kind=jnp.bfloat16):
    values = width * jax.random.normal(rng, extent, jnp.float32)
    if pieces:
        values = values * block_levels(rng, extent, pieces, -0.22, 0.18)
    return jnp.clip(values, -most, most).astype(kind)


def setup_inputs(seed: int = 0) -> dict:
    keys = jax.random.split(jax.random.key(seed), 10)
    tokens = scatter_about(keys[0], (TOKENS, D), 1.0, 6.0, ((0, 256),))
    expert_ids_keys = jax.random.split(jax.random.fold_in(keys[1], 1), TOKENS // TOK_DEV)
    expert_ids_turns = jax.random.permutation(jax.random.fold_in(keys[1], 3), TOKENS // TOK_DEV)
    expert_ids = jax.vmap(lambda own, number: deal_out(jax.random.fold_in(keys[1], 2), own, number, TOK_DEV, EXPERTS, TOPK, CAP, 2))(expert_ids_keys, expert_ids_turns).reshape((TOKENS, TOPK))
    gate_weights = jnp.clip(0.25 + 1.75 * jax.random.uniform(keys[2], (TOKENS, TOPK), jnp.float32) ** block_levels(keys[2], (TOKENS, TOPK), ((0, 256),), -0.2, 0.2), 0.25, 2.0)
    span_ids = draw_span_ids(jax.random.fold_in(keys[9], 71), 0)
    w_gate = scatter_about(keys[4], (EXPERTS, D, FF), D ** -0.5, 0.125, ((0, 32),))
    w_up = scatter_about(keys[5], (EXPERTS, D, FF), D ** -0.5, 0.125, ((0, 32),))
    w_down = scatter_about(keys[6], (EXPERTS, FF, D), FF ** -0.5, 0.21875, ((0, 32),))
    w_proj = scatter_about(keys[7], (D, SD), D ** -0.5, 0.125, ((1, 8),))
    cotangent = scatter_about(keys[8], (N_DP, SPANS_GRP, SD), SPANS ** -0.5, 0.046875, ((1, 32), (2, 8)))
    return dict(tokens=tokens, expert_ids=expert_ids, gate_weights=gate_weights, span_ids=span_ids, w_gate=w_gate, w_up=w_up, w_down=w_down, w_proj=w_proj, cotangent=cotangent)


def slot_table(chosen, experts, cap):
    count, topk = chosen.shape
    hits = (chosen[:, :, None] == jnp.arange(experts, dtype=jnp.int32)[None, None, :]).astype(jnp.int32)
    per_token = jnp.sum(hits, axis=1)
    before = jnp.cumsum(per_token, axis=0) - per_token
    slot = jnp.sum(hits * before[:, None, :], axis=2).astype(jnp.int32)
    owners = jnp.repeat(jnp.arange(count, dtype=jnp.int32), topk)
    table = jnp.full((experts, cap), count, jnp.int32)
    table = table.at[chosen.reshape(-1), slot.reshape(-1)].set(owners)
    return table, slot


def reference(tokens, expert_ids, gate_weights, span_ids, w_gate, w_up, w_down, w_proj, cotangent):
    high = lax.Precision.HIGHEST
    blocks = N_DP * N_EXPERT
    gate32 = w_gate.astype(jnp.float32)
    up32 = w_up.astype(jnp.float32)
    down32 = w_down.astype(jnp.float32)
    tok_blocks = tokens.reshape(blocks, TOK_DEV, D)
    id_blocks = expert_ids.reshape(blocks, TOK_DEV, TOPK)
    weight_blocks = gate_weights.reshape(blocks, TOK_DEV, TOPK)

    def one_block(inputs):
        block_tokens, chosen, weights = inputs
        table, slot = slot_table(chosen, EXPERTS, CAP)
        padded = jnp.concatenate([block_tokens, jnp.zeros((1, D), jnp.bfloat16)], axis=0)
        rows = jnp.take(padded, table, axis=0).astype(jnp.float32)
        gate = jnp.einsum('ecd,edf->ecf', rows, gate32, precision=high)
        upper = jnp.einsum('ecd,edf->ecf', rows, up32, precision=high)
        hidden = (jax.nn.silu(gate) * upper).astype(jnp.bfloat16).astype(jnp.float32)
        result = jnp.einsum('ecf,efd->ecd', hidden, down32, precision=high).astype(jnp.bfloat16)
        flat = result.reshape(EXPERTS * CAP, D)
        picked = jnp.take(flat, chosen * CAP + slot, axis=0).astype(jnp.float32)
        return jnp.einsum('tk,tkd->td', weights, picked, precision=high).astype(jnp.bfloat16)

    combined = lax.map(one_block, (tok_blocks, id_blocks, weight_blocks))
    local_ids = span_ids.reshape(blocks, TOK_DEV)
    onehot = (local_ids[:, None, :] == jnp.arange(SPANS_DEV, dtype=jnp.int32)[None, :, None]).astype(jnp.float32)
    sums = jnp.einsum('bsp,bpd->bsd', onehot, combined.astype(jnp.float32), precision=high)
    counts = jnp.sum(onehot, axis=2)
    pooled = (sums / counts[:, :, None]).astype(jnp.bfloat16)
    pooled = pooled.reshape(N_DP, SPANS_GRP, D)
    pooled32 = pooled.astype(jnp.float32)
    student = jnp.einsum('gsd,dc->gsc', pooled32, w_proj.astype(jnp.float32), precision=high).astype(jnp.bfloat16)
    grad_proj = jnp.einsum('gsd,gsc->dc', pooled32, cotangent.astype(jnp.float32), precision=high)
    return student, grad_proj
```

```python
import jax
import jax.numpy as jnp
from jax import lax
from jax.experimental import pallas as pl
from jax.experimental.pallas import tpu as pltpu
from jax.sharding import PartitionSpec as P

MESH = pl.DeviceIdType.MESH
NZ, NY = 8, 4
CAP = 48
DELTA = (0, -1, 1, -2, 2, -3, 3, 4)
PAIR = (0, 2, 1, 4, 3, 6, 5, 7)
RETURN_ORDER = (5, 6, 7, 3, 4, 1, 2, 0)


def place():
    d = lax.axis_index("dp")
    e = lax.axis_index("expert")
    return d, e // NY, lax.rem(e, NY)


def at_z(d, z, y, dz):
    return (d, lax.rem(z + NZ + dz, NZ) * NY + y)


def at_y(d, z, y, dy):
    return (d, z * NY + lax.rem(y + NY + dy, NY))


def moe_kernel(
    tokens, ids_hbm, gates, spans, wg_hbm, wu_hbm, wd_hbm, pooled,
    ids, wg, wu, wd, slot_t, gate_t, meta_out, meta, zbuf, sbuf, xbuf, hid, rbuf, bbuf,
    qbuf, msg, got, load_sem, meta_ss, meta_rs, z_ss, z_rs, y_ss, y_rs, b_ss, b_rs, c_ss, c_rs,
):
    d, z, y = place()
    e = z * NY + y
    tok, width = tokens.shape
    ff = wg.shape[1]
    spn = pooled.shape[0]
    half_t, half_s = tok // 2, spn // 2

    barrier = pltpu.get_barrier_semaphore()
    for dz in DELTA[1:]:
        pl.semaphore_signal(barrier, inc=1, device_id=at_z(d, z, y, dz), device_id_type=MESH)
    for dy in range(1, NY):
        pl.semaphore_signal(barrier, inc=1, device_id=at_y(d, z, y, dy), device_id_type=MESH)
    ids_copy = pltpu.make_async_copy(ids_hbm.at[pl.ds(e * tok, tok)], ids, load_sem.at[3])
    ids_copy.start()
    loads = [
        pltpu.make_async_copy(src.at[0], dst, load_sem.at[n])
        for n, (src, dst) in enumerate(((wg_hbm, wg), (wu_hbm, wu), (wd_hbm, wd)))
    ]
    for load in loads:
        load.start()
    pl.semaphore_wait(barrier, NZ - 1 + NY - 1)

    def remote(src, dst, ss, rs, dev):
        return pltpu.make_async_remote_copy(
            src_ref=src, dst_ref=dst, send_sem=ss, recv_sem=rs, device_id=dev, device_id_type=MESH
        )

    pending = []

    def z_send(src, dst, s, dz):
        copy = remote(src, dst, z_ss.at[s], z_rs.at[s], at_z(d, z, y, dz))
        copy.start()
        pending.append(copy)

    z_send(tokens, zbuf.at[1], 1, 1)
    z_send(tokens, zbuf.at[2], 2, -1)

    ids_copy.wait()
    lanes = lax.broadcasted_iota(jnp.int32, (tok, 128), 1)
    taken = jnp.zeros((tok, 128), jnp.float32)
    weight = jnp.zeros((tok, 128), jnp.float32)
    for k in range(ids.shape[1]):
        named = ids[:, k : k + 1] == lanes
        taken = taken + jnp.where(named, 1.0, 0.0)
        weight = weight + jnp.where(named, gates[:, k : k + 1], 0.0)
    rows = lax.broadcasted_iota(jnp.int32, (tok, tok), 0)
    cols = lax.broadcasted_iota(jnp.int32, (tok, tok), 1)
    earlier = jnp.where(cols < rows, 1.0, 0.0).astype(jnp.bfloat16)
    before = jnp.dot(earlier, taken.astype(jnp.bfloat16), preferred_element_type=jnp.float32)
    slot_t[...] = jnp.transpose(jnp.where(taken > 0.0, before, -1.0))
    gate_t[...] = jnp.transpose(weight)
    own_span = spans[pl.ds(d, 1), :].astype(jnp.float32)
    meta_copies = []
    for i in range(NZ):
        there = lax.rem(z + NZ + DELTA[i], NZ) * NY
        for j in range(NY):
            row = there + lax.rem(y + j, NY)
            slab = meta if i == 0 else meta_out
            slab[i, j, 0:1, :] = slot_t[pl.ds(row, 1), :]
            slab[i, j, 1:2, :] = gate_t[pl.ds(row, 1), :]
            slab[i, j, 2:3, :] = own_span
        if i > 0:
            copy = remote(
                meta_out.at[i], meta.at[PAIR[i]], meta_ss.at[i], meta_rs.at[PAIR[i]],
                at_z(d, z, y, DELTA[i]),
            )
            copy.start()
            meta_copies.append(copy)

    def meta_wait(i):
        if i > 0:
            remote(meta_out.at[i], meta.at[i], meta_ss.at[i], meta_rs.at[i], (d, e)).wait_recv()

    slots = lax.broadcasted_iota(jnp.int32, (CAP, tok), 0).astype(jnp.float32)

    def onehot(i, j):
        return jnp.where(meta[i, j, 0:1, :] == slots, 1.0, 0.0)

    y_copies = {}

    def dispatch(i):
        block = tokens if i == 0 else zbuf.at[i]
        pick = jnp.concatenate([onehot(i, j) for j in range(NY)], axis=0).astype(jnp.bfloat16)
        tile = 512

        def body(n, carry):
            at = pl.ds(pl.multiple_of(n * tile, tile), tile)
            out = jnp.dot(pick, block[:, at], preferred_element_type=jnp.float32)
            out = out.astype(jnp.bfloat16)
            xbuf[i, 0:CAP, at] = out[0:CAP]
            sbuf[i, :, at] = out[CAP:]
            return carry

        lax.fori_loop(0, width // tile, body, 0)
        for j in range(1, NY):
            back = NY - j
            copy = remote(
                sbuf.at[i, pl.ds((j - 1) * CAP, CAP)], xbuf.at[i, pl.ds(back * CAP, CAP)],
                y_ss.at[i, j], y_rs.at[i, back], at_y(d, z, y, j),
            )
            copy.start()
            y_copies[i, j] = copy

    def ffn(i):
        for j in range(1, NY):
            remote(
                sbuf.at[i, pl.ds((j - 1) * CAP, CAP)], xbuf.at[i, pl.ds(j * CAP, CAP)],
                y_ss.at[i, j], y_rs.at[i, j], (d, e),
            ).wait_recv()
        wide = 256

        def up(n, carry):
            at = pl.ds(pl.multiple_of(n * wide, wide), wide)
            x = xbuf[i]
            g = jnp.dot(x, wg[:, at], preferred_element_type=jnp.float32)
            u = jnp.dot(x, wu[:, at], preferred_element_type=jnp.float32)
            hid[:, at] = (g / (1.0 + jnp.exp(-g)) * u).astype(jnp.bfloat16)
            return carry

        lax.fori_loop(0, ff // wide, up, 0)

        def down(n, carry):
            at = pl.ds(pl.multiple_of(n * wide, wide), wide)
            out = jnp.dot(hid[...], wd[:, at], preferred_element_type=jnp.float32)
            out = out.astype(jnp.bfloat16)
            bbuf[i, 0:CAP, at] = out[0:CAP]
            rbuf[i, :, at] = out[CAP:]
            return carry

        lax.fori_loop(0, width // wide, down, 0)

    b_copies = {}

    def give_back(i):
        for j in range(1, NY):
            back = NY - j
            copy = remote(
                rbuf.at[i, pl.ds((j - 1) * CAP, CAP)], bbuf.at[i, pl.ds(back * CAP, CAP)],
                b_ss.at[i, j], b_rs.at[i, back], at_y(d, z, y, j),
            )
            copy.start()
            b_copies[i, j] = copy

    span_rows = lax.broadcasted_iota(jnp.int32, (spn, tok), 0).astype(jnp.float32)
    last = (((1,), (1,)), ((), ()))

    def pool(i):
        for j in range(1, NY):
            remote(
                rbuf.at[i, pl.ds((j - 1) * CAP, CAP)], bbuf.at[i, pl.ds(j * CAP, CAP)],
                b_ss.at[i, j], b_rs.at[i, j], (d, e),
            ).wait_recv()
        high, low = [], []
        for j in range(NY):
            take = onehot(i, j).astype(jnp.bfloat16)
            share = jnp.where(meta[i, j, 2:3, :] == span_rows, meta[i, j, 1:2, :], 0.0)
            top = share.astype(jnp.bfloat16)
            rest = (share - top.astype(jnp.float32)).astype(jnp.bfloat16)
            high.append(lax.dot_general(top, take, last, preferred_element_type=jnp.float32))
            low.append(lax.dot_general(rest, take, last, preferred_element_type=jnp.float32))
        high = jnp.concatenate(high, axis=1).astype(jnp.bfloat16)
        low = jnp.concatenate(low, axis=1).astype(jnp.bfloat16)
        both = jnp.concatenate([high, low], axis=0)
        tile = 512

        def body(n, carry):
            at = pl.ds(pl.multiple_of(n * tile, tile), tile)
            out = jnp.dot(both, bbuf[i, :, at], preferred_element_type=jnp.float32)
            qbuf[i, :, at] = out[:spn] + out[spn:]
            return carry

        lax.fori_loop(0, width // tile, body, 0)

    chain = []

    def pass_on(way, hop, i):
        if hop == NZ // 2:
            part = pl.ds(way * half_s, half_s)
            msg[way, hop - 1, part, :] = qbuf[i, part, :].astype(jnp.bfloat16)
        else:
            src = remote_got(way, hop)
            src.wait_recv()
            if hop == NZ // 2 - 1:
                part, other = pl.ds(way * half_s, half_s), pl.ds((1 - way) * half_s, half_s)
                msg[way, hop - 1, part, :] = (
                    qbuf[i, part, :] + got[way, hop, part, :].astype(jnp.float32)
                ).astype(jnp.bfloat16)
                msg[way, hop - 1, other, :] = qbuf[i, other, :].astype(jnp.bfloat16)
            else:
                msg[way, hop - 1] = (
                    qbuf[i] + got[way, hop].astype(jnp.float32)
                ).astype(jnp.bfloat16)
        copy = remote(
            chain_part(msg, way, hop - 1), chain_part(got, way, hop - 1),
            c_ss.at[way, hop - 1], c_rs.at[way, hop - 1], at_z(d, z, y, 1 - 2 * way),
        )
        copy.start()
        chain.append(copy)

    def chain_part(buf, way, n):
        if n == NZ // 2 - 1:
            return buf.at[way, n, pl.ds(way * half_s, half_s)]
        return buf.at[way, n]

    def remote_got(way, n):
        return remote(
            chain_part(msg, way, n), chain_part(got, way, n), c_ss.at[way, n], c_rs.at[way, n], (d, e)
        )

    meta_wait(0)
    dispatch(0)

    def z_recv(s, part=None):
        dst = zbuf.at[s] if part is None else zbuf.at[7, pl.ds(part * half_t, half_t)]
        n = s if part is None else 7 + part
        remote(dst, dst, z_ss.at[n], z_rs.at[n], (d, e)).wait_recv()

    for p in (1, 2, 3):
        a, b = 2 * p - 1, 2 * p
        z_recv(a)
        if p < 3:
            z_send(zbuf.at[a], zbuf.at[a + 2], a + 2, 1)
        else:
            part = pl.ds(0, half_t)
            z_send(zbuf.at[a, part], zbuf.at[7, part], 7, 1)
        z_recv(b)
        if p < 3:
            z_send(zbuf.at[b], zbuf.at[b + 2], b + 2, -1)
        else:
            part = pl.ds(half_t, half_t)
            z_send(zbuf.at[b, part], zbuf.at[7, part], 8, -1)
        for i in (a, b):
            meta_wait(i)
            dispatch(i)
        if p == 1:
            for load in loads:
                load.wait()
            ffn(0)
        if p == 3:
            ffn(1)
            ffn(2)
    z_recv(7, 0)
    z_recv(7, 1)
    meta_wait(7)
    dispatch(7)
    for i in (3, 4, 5, 6):
        ffn(i)
    give_back(5)
    give_back(6)
    ffn(7)
    give_back(7)
    for n, i in enumerate(RETURN_ORDER):
        pool(i)
        if n + 3 < NZ:
            give_back(RETURN_ORDER[n + 3])
        if i == 7:
            pass_on(0, 4, 7)
            pass_on(1, 4, 7)
            pass_on(0, 3, 6)
            pass_on(1, 3, 5)
        if i == 4:
            pass_on(0, 2, 4)
            pass_on(1, 2, 3)
        if i == 2:
            pass_on(0, 1, 2)
            pass_on(1, 1, 1)
    count = jnp.sum(jnp.where(own_span == span_rows, 1.0, 0.0), axis=1, keepdims=True)
    remote_got(0, 0).wait_recv()
    remote_got(1, 0).wait_recv()
    total = qbuf[0] + got[0, 0].astype(jnp.float32) + got[1, 0].astype(jnp.float32)
    pooled[...] = (total / count).astype(jnp.bfloat16)
    for copy in pending + meta_copies + list(y_copies.values()) + list(b_copies.values()) + chain:
        copy.wait_send()


def moe(tokens, expert_ids, gate_weights, span_ids, w_gate, w_up, w_down):
    tok, width = tokens.shape
    ff = w_gate.shape[2]
    spn = tok // 2
    vmem = pl.BlockSpec(memory_space=pltpu.VMEM)
    hbm = pl.BlockSpec(memory_space=pl.ANY)
    bf, f32 = jnp.bfloat16, jnp.float32
    dma = pltpu.SemaphoreType.DMA
    return pl.pallas_call(
        moe_kernel,
        out_shape=jax.ShapeDtypeStruct((spn, width), bf),
        in_specs=[vmem, hbm, vmem, vmem, hbm, hbm, hbm],
        out_specs=vmem,
        scratch_shapes=[
            pltpu.VMEM((tok, expert_ids.shape[1]), jnp.int32),
            pltpu.VMEM((width, ff), bf),
            pltpu.VMEM((width, ff), bf),
            pltpu.VMEM((ff, width), bf),
            pltpu.VMEM((128, tok), f32),
            pltpu.VMEM((128, tok), f32),
            pltpu.VMEM((NZ, NY, 8, tok), f32),
            pltpu.VMEM((NZ, NY, 8, tok), f32),
            pltpu.VMEM((NZ, tok, width), bf),
            pltpu.VMEM((NZ, (NY - 1) * CAP, width), bf),
            pltpu.VMEM((NZ, NY * CAP, width), bf),
            pltpu.VMEM((NY * CAP, ff), bf),
            pltpu.VMEM((NZ, (NY - 1) * CAP, width), bf),
            pltpu.VMEM((NZ, NY * CAP, width), bf),
            pltpu.VMEM((NZ, spn, width), f32),
            pltpu.VMEM((2, NZ // 2, spn, width), bf),
            pltpu.VMEM((2, NZ // 2, spn, width), bf),
            dma((4,)),
            dma((NZ,)), dma((NZ,)),
            dma((NZ + 1,)), dma((NZ + 1,)),
            dma((NZ, NY)), dma((NZ, NY)),
            dma((NZ, NY)), dma((NZ, NY)),
            dma((2, NZ // 2)), dma((2, NZ // 2)),
        ],
        compiler_params=pltpu.CompilerParams(
            collective_id=0, has_side_effects=True, vmem_limit_bytes=60 * 2**20
        ),
    )(tokens, expert_ids, gate_weights, span_ids, w_gate, w_up, w_down)


def local(tokens, expert_ids, gate_weights, span_ids, w_gate, w_up, w_down, w_proj, cotangent):
    pooled = moe(tokens, expert_ids, gate_weights, span_ids, w_gate, w_up, w_down)
    pooled_all = lax.all_gather(pooled, "dp", axis=0, tiled=True)
    columns = w_proj.shape[1]
    student = jnp.dot(pooled_all, w_proj, preferred_element_type=jnp.float32).astype(jnp.bfloat16)
    student = student.reshape(cotangent.shape)
    cot_flat = cotangent.reshape(-1, columns)
    grad_proj = lax.psum_scatter(
        lax.dot_general(
            pooled_all, cot_flat, (((0,), (0,)), ((), ())), preferred_element_type=jnp.float32
        ),
        "expert",
        scatter_dimension=0,
        tiled=True,
    )
    return (student, grad_proj)


def solution(mesh):
    placed = (
        P(("dp", "expert"), None),
        P("dp", None),
        P(("dp", "expert"), None),
        P(None, "expert"),
        P("expert", None, None),
        P("expert", None, None),
        P("expert", None, None),
        P(None, "dp"),
        P(None, "expert", "dp"),
    )
    return jax.shard_map(
        local,
        mesh=mesh,
        in_specs=placed,
        out_specs=(P(None, "expert", "dp"), P("expert", "dp")),
        check_vma=False,
    )
```

```python
import jax
import jax.numpy as jnp
from jax import lax
from jax.experimental import pallas as pl
from jax.experimental.pallas import tpu as pltpu
from jax.sharding import PartitionSpec as P

MESH = pl.DeviceIdType.MESH
NZ, NY = 8, 4
CAP = 48
DELTA = (0, -1, 1, -2, 2, -3, 3, 4)
PAIR = (0, 2, 1, 4, 3, 6, 5, 7)
RETURN_ORDER = (5, 6, 7, 3, 4, 1, 2, 0)


def place():
    d = lax.axis_index("dp")
    e = lax.axis_index("expert")
    return d, e // NY, lax.rem(e, NY)


def at_z(d, z, y, dz):
    return (d, lax.rem(z + NZ + dz, NZ) * NY + y)


def at_y(d, z, y, dy):
    return (d, z * NY + lax.rem(y + NY + dy, NY))


def moe_kernel(
    tokens, ids_hbm, gates, spans, wg_hbm, wu_hbm, wd_hbm, pooled,
    ids, wg, wu, wd, slot_t, gate_t, meta_out, meta, zbuf, sbuf, xbuf, hid, rbuf, bbuf,
    qbuf, msg, got, load_sem, meta_ss, meta_rs, z_ss, z_rs, y_ss, y_rs, b_ss, b_rs, c_ss, c_rs,
):
    d, z, y = place()
    e = z * NY + y
    tok, width = tokens.shape
    ff = wg.shape[1]
    spn = pooled.shape[0]
    half_t, half_s = tok // 2, spn // 2

    barrier = pltpu.get_barrier_semaphore()
    for dz in DELTA[1:]:
        pl.semaphore_signal(barrier, inc=1, device_id=at_z(d, z, y, dz), device_id_type=MESH)
    for dy in range(1, NY):
        pl.semaphore_signal(barrier, inc=1, device_id=at_y(d, z, y, dy), device_id_type=MESH)
    ids_copy = pltpu.make_async_copy(ids_hbm.at[:, pl.ds(pl.multiple_of(e * tok, tok), tok)], ids, load_sem.at[3])
    ids_copy.start()
    loads = [
        pltpu.make_async_copy(src.at[0], dst, load_sem.at[n])
        for n, (src, dst) in enumerate(((wg_hbm, wg), (wu_hbm, wu), (wd_hbm, wd)))
    ]
    for load in loads:
        load.start()
    pl.semaphore_wait(barrier, NZ - 1 + NY - 1)

    def remote(src, dst, ss, rs, dev):
        return pltpu.make_async_remote_copy(
            src_ref=src, dst_ref=dst, send_sem=ss, recv_sem=rs, device_id=dev, device_id_type=MESH
        )

    pending = []

    def z_send(src, dst, s, dz):
        copy = remote(src, dst, z_ss.at[s], z_rs.at[s], at_z(d, z, y, dz))
        copy.start()
        pending.append(copy)

    z_send(tokens, zbuf.at[1], 1, 1)
    z_send(tokens, zbuf.at[2], 2, -1)

    ids_copy.wait()
    experts = NZ * NY
    number = lax.broadcasted_iota(jnp.int32, (experts, tok), 0)
    taken = jnp.zeros((experts, tok), jnp.float32)
    weight = jnp.zeros((experts, tok), jnp.float32)
    for k in range(ids.shape[0]):
        named = ids[k : k + 1, :] == number
        taken = taken + jnp.where(named, 1.0, 0.0)
        weight = weight + jnp.where(named, gates[k : k + 1, :], 0.0)
    rows = lax.broadcasted_iota(jnp.int32, (tok, tok), 0)
    cols = lax.broadcasted_iota(jnp.int32, (tok, tok), 1)
    earlier = jnp.where(rows < cols, 1.0, 0.0).astype(jnp.bfloat16)
    before = jnp.dot(taken.astype(jnp.bfloat16), earlier, preferred_element_type=jnp.float32)
    slot_t[...] = jnp.where(taken > 0.0, before, -1.0)
    gate_t[...] = weight
    own_span = spans[pl.ds(d, 1), :].astype(jnp.float32)
    meta_copies = []
    for i in range(NZ):
        there = lax.rem(z + NZ + DELTA[i], NZ) * NY
        for j in range(NY):
            row = there + lax.rem(y + j, NY)
            slab = meta if i == 0 else meta_out
            slab[i, j, 0:1, :] = slot_t[pl.ds(row, 1), :]
            slab[i, j, 1:2, :] = gate_t[pl.ds(row, 1), :]
            slab[i, j, 2:3, :] = own_span
        if i > 0:
            copy = remote(
                meta_out.at[i], meta.at[PAIR[i]], meta_ss.at[i], meta_rs.at[PAIR[i]],
                at_z(d, z, y, DELTA[i]),
            )
            copy.start()
            meta_copies.append(copy)

    def meta_wait(i):
        if i > 0:
            remote(meta_out.at[i], meta.at[i], meta_ss.at[i], meta_rs.at[i], (d, e)).wait_recv()

    slots = lax.broadcasted_iota(jnp.int32, (CAP, tok), 0).astype(jnp.float32)

    def onehot(i, j):
        return jnp.where(meta[i, j, 0:1, :] == slots, 1.0, 0.0)

    y_copies = {}

    def dispatch(i):
        block = tokens if i == 0 else zbuf.at[i]
        pick = jnp.concatenate([onehot(i, j) for j in range(NY)], axis=0).astype(jnp.bfloat16)
        tile = 512

        def body(n, carry):
            at = pl.ds(pl.multiple_of(n * tile, tile), tile)
            out = jnp.dot(pick, block[:, at], preferred_element_type=jnp.float32)
            out = out.astype(jnp.bfloat16)
            xbuf[i, 0:CAP, at] = out[0:CAP]
            sbuf[i, :, at] = out[CAP:]
            return carry

        lax.fori_loop(0, width // tile, body, 0)
        for j in range(1, NY):
            back = NY - j
            copy = remote(
                sbuf.at[i, pl.ds((j - 1) * CAP, CAP)], xbuf.at[i, pl.ds(back * CAP, CAP)],
                y_ss.at[i, j], y_rs.at[i, back], at_y(d, z, y, j),
            )
            copy.start()
            y_copies[i, j] = copy

    def ffn(i):
        for j in range(1, NY):
            remote(
                sbuf.at[i, pl.ds((j - 1) * CAP, CAP)], xbuf.at[i, pl.ds(j * CAP, CAP)],
                y_ss.at[i, j], y_rs.at[i, j], (d, e),
            ).wait_recv()
        wide = 256

        def up(n, carry):
            at = pl.ds(pl.multiple_of(n * wide, wide), wide)
            x = xbuf[i]
            g = jnp.dot(x, wg[:, at], preferred_element_type=jnp.float32)
            u = jnp.dot(x, wu[:, at], preferred_element_type=jnp.float32)
            hid[:, at] = (g / (1.0 + jnp.exp(-g)) * u).astype(jnp.bfloat16)
            return carry

        lax.fori_loop(0, ff // wide, up, 0)

        def down(n, carry):
            at = pl.ds(pl.multiple_of(n * wide, wide), wide)
            out = jnp.dot(hid[...], wd[:, at], preferred_element_type=jnp.float32)
            out = out.astype(jnp.bfloat16)
            bbuf[i, 0:CAP, at] = out[0:CAP]
            rbuf[i, :, at] = out[CAP:]
            return carry

        lax.fori_loop(0, width // wide, down, 0)

    b_copies = {}

    def give_back(i):
        for j in range(1, NY):
            back = NY - j
            copy = remote(
                rbuf.at[i, pl.ds((j - 1) * CAP, CAP)], bbuf.at[i, pl.ds(back * CAP, CAP)],
                b_ss.at[i, j], b_rs.at[i, back], at_y(d, z, y, j),
            )
            copy.start()
            b_copies[i, j] = copy

    span_rows = lax.broadcasted_iota(jnp.int32, (spn, tok), 0).astype(jnp.float32)
    last = (((1,), (1,)), ((), ()))

    def pool(i):
        for j in range(1, NY):
            remote(
                rbuf.at[i, pl.ds((j - 1) * CAP, CAP)], bbuf.at[i, pl.ds(j * CAP, CAP)],
                b_ss.at[i, j], b_rs.at[i, j], (d, e),
            ).wait_recv()
        high, low = [], []
        for j in range(NY):
            take = onehot(i, j).astype(jnp.bfloat16)
            share = jnp.where(meta[i, j, 2:3, :] == span_rows, meta[i, j, 1:2, :], 0.0)
            top = share.astype(jnp.bfloat16)
            rest = (share - top.astype(jnp.float32)).astype(jnp.bfloat16)
            high.append(lax.dot_general(top, take, last, preferred_element_type=jnp.float32))
            low.append(lax.dot_general(rest, take, last, preferred_element_type=jnp.float32))
        high = jnp.concatenate(high, axis=1).astype(jnp.bfloat16)
        low = jnp.concatenate(low, axis=1).astype(jnp.bfloat16)
        both = jnp.concatenate([high, low], axis=0)
        tile = 512

        def body(n, carry):
            at = pl.ds(pl.multiple_of(n * tile, tile), tile)
            out = jnp.dot(both, bbuf[i, :, at], preferred_element_type=jnp.float32)
            qbuf[i, :, at] = out[:spn] + out[spn:]
            return carry

        lax.fori_loop(0, width // tile, body, 0)

    chain = []

    def pass_on(way, hop, i):
        if hop == NZ // 2:
            part = pl.ds(way * half_s, half_s)
            msg[way, hop - 1, part, :] = qbuf[i, part, :].astype(jnp.bfloat16)
        else:
            src = remote_got(way, hop)
            src.wait_recv()
            if hop == NZ // 2 - 1:
                part, other = pl.ds(way * half_s, half_s), pl.ds((1 - way) * half_s, half_s)
                msg[way, hop - 1, part, :] = (
                    qbuf[i, part, :] + got[way, hop, part, :].astype(jnp.float32)
                ).astype(jnp.bfloat16)
                msg[way, hop - 1, other, :] = qbuf[i, other, :].astype(jnp.bfloat16)
            else:
                msg[way, hop - 1] = (
                    qbuf[i] + got[way, hop].astype(jnp.float32)
                ).astype(jnp.bfloat16)
        copy = remote(
            chain_part(msg, way, hop - 1), chain_part(got, way, hop - 1),
            c_ss.at[way, hop - 1], c_rs.at[way, hop - 1], at_z(d, z, y, 1 - 2 * way),
        )
        copy.start()
        chain.append(copy)

    def chain_part(buf, way, n):
        if n == NZ // 2 - 1:
            return buf.at[way, n, pl.ds(way * half_s, half_s)]
        return buf.at[way, n]

    def remote_got(way, n):
        return remote(
            chain_part(msg, way, n), chain_part(got, way, n), c_ss.at[way, n], c_rs.at[way, n], (d, e)
        )

    meta_wait(0)
    dispatch(0)

    def z_recv(s, part=None):
        dst = zbuf.at[s] if part is None else zbuf.at[7, pl.ds(part * half_t, half_t)]
        n = s if part is None else 7 + part
        remote(dst, dst, z_ss.at[n], z_rs.at[n], (d, e)).wait_recv()

    for p in (1, 2, 3):
        a, b = 2 * p - 1, 2 * p
        z_recv(a)
        if p < 3:
            z_send(zbuf.at[a], zbuf.at[a + 2], a + 2, 1)
        else:
            part = pl.ds(0, half_t)
            z_send(zbuf.at[a, part], zbuf.at[7, part], 7, 1)
        z_recv(b)
        if p < 3:
            z_send(zbuf.at[b], zbuf.at[b + 2], b + 2, -1)
        else:
            part = pl.ds(half_t, half_t)
            z_send(zbuf.at[b, part], zbuf.at[7, part], 8, -1)
        for i in (a, b):
            meta_wait(i)
            dispatch(i)
        if p == 1:
            for load in loads:
                load.wait()
            ffn(0)
        if p == 3:
            ffn(1)
            ffn(2)
    z_recv(7, 0)
    z_recv(7, 1)
    meta_wait(7)
    dispatch(7)
    for i in (3, 4, 5, 6):
        ffn(i)
    give_back(5)
    give_back(6)
    ffn(7)
    give_back(7)
    for n, i in enumerate(RETURN_ORDER):
        pool(i)
        if n + 3 < NZ:
            give_back(RETURN_ORDER[n + 3])
        if i == 7:
            pass_on(0, 4, 7)
            pass_on(1, 4, 7)
            pass_on(0, 3, 6)
            pass_on(1, 3, 5)
        if i == 4:
            pass_on(0, 2, 4)
            pass_on(1, 2, 3)
        if i == 2:
            pass_on(0, 1, 2)
            pass_on(1, 1, 1)
    count = jnp.sum(jnp.where(own_span == span_rows, 1.0, 0.0), axis=1, keepdims=True)
    remote_got(0, 0).wait_recv()
    remote_got(1, 0).wait_recv()
    total = qbuf[0] + got[0, 0].astype(jnp.float32) + got[1, 0].astype(jnp.float32)
    pooled[...] = (total / count).astype(jnp.bfloat16)
    for copy in pending + meta_copies + list(y_copies.values()) + list(b_copies.values()) + chain:
        copy.wait_send()


def moe(tokens, expert_ids, gate_weights, span_ids, w_gate, w_up, w_down):
    tok, width = tokens.shape
    ff = w_gate.shape[2]
    spn = tok // 2
    vmem = pl.BlockSpec(memory_space=pltpu.VMEM)
    hbm = pl.BlockSpec(memory_space=pl.ANY)
    bf, f32 = jnp.bfloat16, jnp.float32
    dma = pltpu.SemaphoreType.DMA
    return pl.pallas_call(
        moe_kernel,
        out_shape=jax.ShapeDtypeStruct((spn, width), bf),
        in_specs=[vmem, hbm, vmem, vmem, hbm, hbm, hbm],
        out_specs=vmem,
        scratch_shapes=[
            pltpu.VMEM((expert_ids.shape[1], tok), jnp.int32),
            pltpu.VMEM((width, ff), bf),
            pltpu.VMEM((width, ff), bf),
            pltpu.VMEM((ff, width), bf),
            pltpu.VMEM((NZ * NY, tok), f32),
            pltpu.VMEM((NZ * NY, tok), f32),
            pltpu.VMEM((NZ, NY, 8, tok), f32),
            pltpu.VMEM((NZ, NY, 8, tok), f32),
            pltpu.VMEM((NZ, tok, width), bf),
            pltpu.VMEM((NZ, (NY - 1) * CAP, width), bf),
            pltpu.VMEM((NZ, NY * CAP, width), bf),
            pltpu.VMEM((NY * CAP, ff), bf),
            pltpu.VMEM((NZ, (NY - 1) * CAP, width), bf),
            pltpu.VMEM((NZ, NY * CAP, width), bf),
            pltpu.VMEM((NZ, spn, width), f32),
            pltpu.VMEM((2, NZ // 2, spn, width), bf),
            pltpu.VMEM((2, NZ // 2, spn, width), bf),
            dma((4,)),
            dma((NZ,)), dma((NZ,)),
            dma((NZ + 1,)), dma((NZ + 1,)),
            dma((NZ, NY)), dma((NZ, NY)),
            dma((NZ, NY)), dma((NZ, NY)),
            dma((2, NZ // 2)), dma((2, NZ // 2)),
        ],
        compiler_params=pltpu.CompilerParams(
            collective_id=0, has_side_effects=True, vmem_limit_bytes=60 * 2**20
        ),
    )(tokens, expert_ids.T, gate_weights.T, span_ids, w_gate, w_up, w_down)


def at_x(d, e, dx):
    return (lax.rem(d + 8 + 2 * dx, 8), e)


def pack(g):
    half = g.shape[0] // 2
    tail = jnp.concatenate([g[:half, 256:], g[half:, 256:]], axis=1)
    return jnp.concatenate([g[:, :128], g[:, 128:256], tail], axis=0)


def unpack(p, rows):
    half = rows // 2
    tail = p[2 * rows :]
    tail = jnp.concatenate([tail[:, :64], tail[:, 64:]], axis=0)
    return jnp.concatenate([p[:rows], p[rows : 2 * rows], tail], axis=1)


def project_kernel(
    pooled, w_proj, cot, student, grad,
    everyone, part, part_in, summed, summed_in,
    x_ss, x_rs, s_ss, s_rs, y_ss, y_rs, z_ss, z_rs,
):
    d, z, y = place()
    e = z * NY + y
    x, core = d // 2, lax.rem(d, 2)
    sibling = (2 * x + 1 - core, e)
    spn, width = pooled.shape
    rows = grad.shape[0]
    band = NY * rows

    barrier = pltpu.get_barrier_semaphore()
    for dx in range(1, 4):
        pl.semaphore_signal(barrier, inc=1, device_id=at_x(d, e, dx), device_id_type=MESH)
    pl.semaphore_signal(barrier, inc=1, device_id=sibling, device_id_type=MESH)
    for dz in DELTA[1:]:
        pl.semaphore_signal(barrier, inc=1, device_id=at_z(d, z, y, dz), device_id_type=MESH)
    for dy in range(1, NY):
        pl.semaphore_signal(barrier, inc=1, device_id=at_y(d, z, y, dy), device_id_type=MESH)
    everyone[d] = pooled[...]
    pl.semaphore_wait(barrier, 3 + 1 + NZ - 1 + NY - 1)

    def remote(src, dst, ss, rs, dev):
        return pltpu.make_async_remote_copy(
            src_ref=src, dst_ref=dst, send_sem=ss, recv_sem=rs, device_id=dev, device_id_type=MESH
        )

    started = []

    def send(*what):
        copy = remote(*what)
        copy.start()
        started.append(copy)

    mine = everyone.at[d]
    for dx in (1, 3, 2):
        send(mine, mine, x_ss.at[dx], x_rs.at[4 - dx], at_x(d, e, dx))
    send(mine, mine, s_ss.at[0], s_rs.at[0], sibling)
    for dx in (1, 3, 2):
        block = everyone.at[lax.rem(d + 2 * dx, 8)]
        remote(block, block, x_ss.at[dx], x_rs.at[dx], (d, e)).wait_recv()
        send(block, block, s_ss.at[dx], s_rs.at[dx], sibling)
    for dx in (0, 1, 3, 2):
        block = everyone.at[lax.rem(2 * (x + dx) + 1 - core, 8)]
        remote(block, block, s_ss.at[dx], s_rs.at[dx], (d, e)).wait_recv()

    groups = cot.shape[0]
    order = (7, 5, 6, 3, 4, 1, 2, 0)
    cot_all = cot[...].reshape(groups * spn, cot.shape[2])
    for i in order:
        there = lax.rem(z + NZ + DELTA[i], NZ)
        at = pl.ds(pl.multiple_of(there * band, band), band)
        lhs = everyone[:, :, at].reshape(groups * spn, band)
        out = lax.dot_general(
            lhs, cot_all, (((0,), (0,)), ((), ())), preferred_element_type=jnp.float32
        ).astype(jnp.bfloat16)
        for q in range(NY):
            part[i, q] = pack(out[q * rows : (q + 1) * rows])
        for j in range(1, NY):
            send(
                part.at[i, lax.rem(y + j, NY)], part_in.at[i, NY - j],
                y_ss.at[i, j], y_rs.at[i, NY - j], at_y(d, z, y, j),
            )

    def body(n, carry):
        g = 2 * n
        out = lax.dot_general(
            everyone[pl.ds(g, 2)].reshape(2 * spn, width), w_proj[...],
            (((1,), (1,)), ((), ())), preferred_element_type=jnp.float32,
        ).astype(jnp.bfloat16)
        student[pl.ds(g, 2)] = out.reshape(2, spn, out.shape[1])
        return carry

    lax.fori_loop(0, groups // 2, body, 0)

    for i in order:
        for j in range(1, NY):
            remote(
                part.at[i, j], part_in.at[i, j], y_ss.at[i, j], y_rs.at[i, j], (d, e)
            ).wait_recv()
        total = part[i, y].astype(jnp.float32)
        for j in range(1, NY):
            total = total + part_in[i, j].astype(jnp.float32)
        if i > 0:
            summed[i] = total.astype(jnp.bfloat16)
            send(
                summed.at[i], summed_in.at[PAIR[i]], z_ss.at[i], z_rs.at[PAIR[i]],
                at_z(d, z, y, DELTA[i]),
            )
    for i in order[:-1]:
        remote(summed.at[i], summed_in.at[i], z_ss.at[i], z_rs.at[i], (d, e)).wait_recv()
        total = total + summed_in[i].astype(jnp.float32)
    grad[...] = unpack(total, rows)
    for copy in started:
        copy.wait_send()


def project(pooled, w_proj, cotangent):
    groups, spn, columns = cotangent.shape
    width = pooled.shape[1]
    rows = width // (NZ * NY)
    vmem = pl.BlockSpec(memory_space=pltpu.VMEM)
    bf = jnp.bfloat16
    dma = pltpu.SemaphoreType.DMA
    packed = (rows * columns // 128, 128)
    return pl.pallas_call(
        project_kernel,
        out_shape=(
            jax.ShapeDtypeStruct((groups, spn, columns), bf),
            jax.ShapeDtypeStruct((rows, columns), jnp.float32),
        ),
        in_specs=[vmem] * 3,
        out_specs=(vmem, vmem),
        scratch_shapes=[
            pltpu.VMEM((groups, spn, width), bf),
            pltpu.VMEM((NZ, NY) + packed, bf),
            pltpu.VMEM((NZ, NY) + packed, bf),
            pltpu.VMEM((NZ,) + packed, bf),
            pltpu.VMEM((NZ,) + packed, bf),
            dma((4,)), dma((4,)), dma((4,)), dma((4,)),
            dma((NZ, NY)), dma((NZ, NY)), dma((NZ,)), dma((NZ,)),
        ],
        compiler_params=pltpu.CompilerParams(
            collective_id=1, has_side_effects=True, vmem_limit_bytes=60 * 2**20
        ),
    )(pooled, w_proj.T, cotangent)


def local(tokens, expert_ids, gate_weights, span_ids, w_gate, w_up, w_down, w_proj, cotangent):
    pooled = moe(tokens, expert_ids, gate_weights, span_ids, w_gate, w_up, w_down)
    return project(pooled, w_proj, cotangent)


def solution(mesh):
    placed = (
        P(("dp", "expert"), None),
        P("dp", None),
        P(("dp", "expert"), None),
        P(None, "expert"),
        P("expert", None, None),
        P("expert", None, None),
        P("expert", None, None),
        P(None, "dp"),
        P(None, "expert", "dp"),
    )
    return jax.shard_map(
        local,
        mesh=mesh,
        in_specs=placed,
        out_specs=(P(None, "expert", "dp"), P("expert", "dp")),
        check_vma=False,
    )
```

```python
import jax
import jax.numpy as jnp
from jax import lax
from jax.experimental import pallas as pl
from jax.experimental.pallas import tpu as pltpu
from jax.sharding import PartitionSpec as P

MESH = pl.DeviceIdType.MESH
NX, NZ, NY = 4, 8, 4
CAP = 48
DELTA = (0, -1, 1, -2, 2, -3, 3, 4)
PAIR = (0, 2, 1, 4, 3, 6, 5, 7)
HOP = {4: (7, 7), 3: (6, 5), 2: (4, 3), 1: (2, 1)}
TILE = 256
WIDE = 512
ZA, YA, ZB, YB = 0, 1, 2, 3
COL = (0, 1024, 512, 1536)
OFF = (0, 0, 512, 512)
ON_Z = (True, False, True, False)
META, MY, Z, Y, B, CZ, CY, F, X, S, GY, GZ = range(12)


def place():
    d = lax.axis_index("dp")
    e = lax.axis_index("expert")
    return d, e // NY, lax.rem(e, NY)


def pack(g):
    half = g.shape[0] // 2
    tail = jnp.concatenate([g[:half, 256:], g[half:, 256:]], axis=1)
    return jnp.concatenate([g[:, :128], g[:, 128:256], tail], axis=0)


def unpack(p, rows):
    tail = p[2 * rows :]
    tail = jnp.concatenate([tail[:, :64], tail[:, 64:]], axis=0)
    return jnp.concatenate([p[:rows], p[rows : 2 * rows], tail], axis=1)


def kernel(
    tokens, ids_hbm, gates, spans, wg_hbm, wu_hbm, wd_hbm, proj_hbm, cot_hbm, student, grad,
    ids, wg, wu, wd, w_proj, cot, slot_t, gate_t, lines, meta_out, meta, meta_y, mix_y, mix_z,
    zbuf, sbuf, xbuf, hid, rbuf, bbuf, msg_y, got_y, msg_z, got_z, fin_out, fin_in,
    everyone, acc, part, part_in, summed, summed_in, own_sum,
    load_sem, send_sem, meta_rs, my_rs, z_rs, y_rs, b_rs, c_rs, f_rs, x_rs, s_rs, gy_rs, gz_rs,
):
    d, z, y = place()
    e = z * NY + y
    x, core = d // 2, lax.rem(d, 2)
    me = (d, e)
    sibling = (2 * x + 1 - core, e)
    tok, width = tokens.shape
    ff = wg.shape[1]
    groups, spn, columns = cot.shape
    rows = grad.shape[0]
    f32, bf = jnp.float32, jnp.bfloat16

    def at_z(dz):
        return (d, lax.rem(z + NZ + dz, NZ) * NY + y)

    def at_y(dy):
        return (d, z * NY + lax.rem(y + NY + dy, NY))

    def at_x(dx):
        return (lax.rem(d + 2 * NX + 2 * dx, 2 * NX), e)

    barrier = pltpu.get_barrier_semaphore()
    peers = [at_z(dz) for dz in DELTA[1:]]
    peers += [at_y(dy) for dy in range(1, NY)]
    peers += [at_x(dx) for dx in range(1, NX)] + [sibling]
    for peer in peers:
        pl.semaphore_signal(barrier, inc=1, device_id=peer, device_id_type=MESH)
    ids_copy = pltpu.make_async_copy(
        ids_hbm.at[:, pl.ds(pl.multiple_of(e * tok, tok), tok)], ids, load_sem.at[0]
    )
    ids_copy.start()
    loads = [
        pltpu.make_async_copy(src, dst, load_sem.at[n + 1])
        for n, (src, dst) in enumerate(
            (
                (wg_hbm.at[0], wg),
                (wu_hbm.at[0], wu),
                (wd_hbm.at[0], wd),
                (proj_hbm, w_proj),
                (cot_hbm, cot),
            )
        )
    ]
    for load in loads:
        load.start()
    def remote(src, dst, ss, rs, dev):
        return pltpu.make_async_remote_copy(
            src_ref=src, dst_ref=dst, send_sem=ss, recv_sem=rs, device_id=dev, device_id_type=MESH
        )

    def send(src, dst, kind, rs, dev):
        remote(src, dst, send_sem.at[kind], rs, dev).start()

    def sent(src, kind):
        remote(src, src, send_sem.at[kind], load_sem.at[0], me).wait_send()

    def arrive(dst, rs):
        remote(dst, dst, send_sem.at[0], rs, me).wait_recv()

    half = [pl.ds(h * (width // 2), width // 2) for h in (0, 1)]

    def z_send(src, s, h, dz):
        send(src.at[:, half[h]], zbuf.at[s, :, half[h]], Z, z_rs.at[s, h], at_z(dz))

    def z_recv(s, h):
        arrive(zbuf.at[s, :, half[h]], z_rs.at[s, h])

    ids_copy.wait()
    experts = NZ * NY
    number = lax.broadcasted_iota(jnp.int32, (experts, tok), 0)
    taken = jnp.zeros((experts, tok), f32)
    weight = jnp.zeros((experts, tok), f32)
    for k in range(ids.shape[0]):
        named = ids[k : k + 1, :] == number
        taken = taken + jnp.where(named, 1.0, 0.0)
        weight = weight + jnp.where(named, gates[k : k + 1, :], 0.0)
    row = lax.broadcasted_iota(jnp.int32, (tok, tok), 0)
    col = lax.broadcasted_iota(jnp.int32, (tok, tok), 1)
    earlier = jnp.where(row < col, 1.0, 0.0).astype(bf)
    before = jnp.dot(taken.astype(bf), earlier, preferred_element_type=f32)
    slot_t[...] = jnp.where(taken > 0.0, before, -1.0)
    gate_t[...] = weight
    own_span = spans[pl.ds(d, 1), :].astype(f32)
    lines[...] = jnp.zeros(lines.shape, f32)
    for i in range(NZ):
        there = lax.rem(z + NZ + DELTA[i], NZ) * NY
        for j in range(NY):
            line = there + lax.rem(y + j, NY)
            lines[i, j : j + 1, :] = slot_t[pl.ds(line, 1), :]
            lines[i, NY + j : NY + j + 1, :] = gate_t[pl.ds(line, 1), :]
        lines[i, 2 * NY : 2 * NY + 1, :] = own_span
        if i == 0:
            meta[0] = lines[0].astype(bf)
        else:
            meta_out[i] = lines[i].astype(bf)
    pl.semaphore_wait(barrier, len(peers))
    for i in range(1, NZ):
        send(meta_out.at[i], meta.at[PAIR[i]], META, meta_rs.at[0], at_z(DELTA[i]))
    for h in (0, 1):
        z_send(tokens, 1, h, 1)
        z_send(tokens, 2, h, -1)

    slots = lax.broadcasted_iota(jnp.int32, (CAP, tok), 0).astype(f32)
    span_rows = lax.broadcasted_iota(jnp.int32, (spn, tok), 0).astype(f32)
    last = (((1,), (1,)), ((), ()))

    def onehot(slab, j):
        return jnp.where(slab[j : j + 1, :] == slots, 1.0, 0.0).astype(bf)

    def dispatch(i, h):
        block = tokens if i == 0 else zbuf.at[i]
        slab = meta[i].astype(f32)
        pick = jnp.concatenate([onehot(slab, j) for j in range(NY)], axis=0)

        def body(n, carry):
            at = pl.ds(pl.multiple_of(h * (width // 2) + n * 512, 512), 512)
            out = jnp.dot(pick, block[:, at], preferred_element_type=f32).astype(bf)
            xbuf[i, 0:CAP, at] = out[0:CAP]
            sbuf[i, :, at] = out[CAP:]
            return carry

        lax.fori_loop(0, width // 1024, body, 0)
        for j in range(1, NY):
            back = NY - j
            send(
                sbuf.at[i, pl.ds((j - 1) * CAP, CAP), half[h]],
                xbuf.at[i, pl.ds(back * CAP, CAP), half[h]],
                Y, y_rs.at[i], at_y(j),
            )

    def ffn(i):
        arrive(xbuf.at[i, pl.ds(CAP, (NY - 1) * CAP)], y_rs.at[i])

        def up(n, carry):
            at = pl.ds(pl.multiple_of(n * TILE, TILE), TILE)
            rows_in = xbuf[i]
            g = jnp.dot(rows_in, wg[:, at], preferred_element_type=f32)
            u = jnp.dot(rows_in, wu[:, at], preferred_element_type=f32)
            hid[:, at] = (g / (1.0 + jnp.exp(-g)) * u).astype(bf)
            return carry

        lax.fori_loop(0, ff // TILE, up, 0)
        for c in range(4):

            def down(n, carry):
                at = pl.ds(pl.multiple_of(COL[c] + n * TILE, TILE), TILE)
                out = jnp.dot(hid[...], wd[:, at], preferred_element_type=f32).astype(bf)
                rbuf[i, :, at] = out
                if not ON_Z[c]:
                    own = pl.ds(pl.multiple_of(OFF[c] + n * TILE, TILE), TILE)
                    bbuf[i, 0:CAP, own] = out[0:CAP]
                return carry

            lax.fori_loop(0, WIDE // TILE, down, 0)

    def pooling(slab, j):
        gate = slab[NY + j : NY + j + 1, :]
        share = jnp.where(slab[2 * NY : 2 * NY + 1, :] == span_rows, gate, 0.0).astype(bf)
        out = lax.dot_general(share, onehot(slab, j), last, preferred_element_type=f32)
        return out.astype(bf)

    def mixing(i):
        own = meta[i].astype(f32)
        mix_y[i] = jnp.concatenate([pooling(own, j) for j in range(NY)], axis=1)
        for j in range(NY):
            slab = own if j == 0 else meta_y[j, i].astype(f32)
            mine = pooling(slab, (NY - j) % NY)
            pieces = [mine if q == j else jnp.zeros((spn, CAP), bf) for q in range(NY)]
            mix_z[i, j * spn : (j + 1) * spn] = jnp.concatenate(pieces, axis=1)

    def give_back(c, i):
        src = pl.ds(COL[c], WIDE)
        dst = pl.ds(OFF[c], WIDE)
        for j in range(1, NY):
            back = NY - j
            send(
                rbuf.at[i, pl.ds(j * CAP, CAP), src], bbuf.at[i, pl.ds(back * CAP, CAP), dst],
                B, b_rs.at[c // 2, i], at_y(j),
            )

    def returned(c, i):
        arrive(
            bbuf.at[i, pl.ds(CAP, (NY - 1) * CAP), pl.ds(OFF[c], WIDE)], b_rs.at[c // 2, i]
        )

    def term(c, i, n, part_rows=None):
        mix = mix_z.at[i] if ON_Z[c] else mix_y.at[i]
        mix = mix[...] if part_rows is None else mix[part_rows, :]
        if ON_Z[c]:
            block = rbuf[i, :, pl.ds(COL[c] + n * TILE, TILE)]
        else:
            block = bbuf[i, :, pl.ds(OFF[c] + n * TILE, TILE)]
        return jnp.dot(mix, block, preferred_element_type=f32)

    def chain_part(buf, c, way, hop):
        at = pl.ds(OFF[c], WIDE)
        total = buf.shape[2]
        if hop == NZ // 2:
            return buf.at[way, hop - 1, pl.ds(way * (total // 2), total // 2), at]
        return buf.at[way, hop - 1, :, at]

    def chain_recv(c, way, hop):
        got = got_z if ON_Z[c] else got_y
        arrive(chain_part(got, c, way, hop), c_rs.at[c, way, hop - 1])

    def pass_on(c, hop):
        msg, got = (msg_z, got_z) if ON_Z[c] else (msg_y, got_y)
        half = msg.shape[2] // 2
        for way in (0, 1):
            i = HOP[hop][way]
            if not ON_Z[c] and not (hop == 4 and way == 1):
                returned(c, i)
            if hop < 4:
                chain_recv(c, way, hop + 1)
            side, other = pl.ds(way * half, half), pl.ds((1 - way) * half, half)
            for n in range(WIDE // TILE):
                at = pl.ds(OFF[c] + n * TILE, TILE)
                if hop == 4:
                    msg[way, 3, side, at] = term(c, i, n, side).astype(bf)
                elif hop == 3:
                    came = got[way, 3, side, at].astype(f32)
                    msg[way, 2, side, at] = (term(c, i, n, side) + came).astype(bf)
                    msg[way, 2, other, at] = term(c, i, n, other).astype(bf)
                else:
                    came = got[way, hop, :, at].astype(f32)
                    msg[way, hop - 1, :, at] = (term(c, i, n) + came).astype(bf)
            send(
                chain_part(msg, c, way, hop), chain_part(got, c, way, hop),
                CZ if ON_Z[c] else CY, c_rs.at[c, way, hop - 1], at_z(1 - 2 * way),
            )

    count = jnp.sum(jnp.where(own_span == span_rows, 1.0, 0.0), axis=1, keepdims=True)

    def spread(c):
        mine = everyone.at[d, :, pl.ds(COL[c], WIDE)]
        for dx in (1, 3, 2):
            send(mine, mine, X, x_rs.at[c], at_x(dx))
        send(mine, mine, S, s_rs.at[c], sibling)

    def finish_z(c):
        chain_recv(c, 0, 1)
        chain_recv(c, 1, 1)
        for n in range(WIDE // TILE):
            at = pl.ds(OFF[c] + n * TILE, TILE)
            total = term(c, 0, n) + got_z[0, 0, :, at].astype(f32) + got_z[1, 0, :, at].astype(f32)
            fin_out[:, :, at] = total.astype(bf).reshape(NY, spn, TILE)
        at = pl.ds(OFF[c], WIDE)
        for j in range(1, NY):
            send(
                fin_out.at[j, :, at], fin_in.at[NY - j, :, at],
                F, f_rs.at[c // 2], at_y(j),
            )

    def finish_z_pooled(c):
        at = pl.ds(OFF[c], WIDE)
        total = fin_out[0, :, at].astype(f32)
        arrive(fin_in.at[pl.ds(1, NY - 1), :, at], f_rs.at[c // 2])
        for j in range(1, NY):
            total = total + fin_in[j, :, at].astype(f32)
        everyone[d, :, pl.ds(COL[c], WIDE)] = (total / count).astype(bf)
        spread(c)

    def finish_y(c):
        returned(c, 0)
        chain_recv(c, 0, 1)
        chain_recv(c, 1, 1)
        for n in range(WIDE // TILE):
            at = pl.ds(OFF[c] + n * TILE, TILE)
            total = term(c, 0, n) + got_y[0, 0, :, at].astype(f32) + got_y[1, 0, :, at].astype(f32)
            everyone[d, :, pl.ds(COL[c] + n * TILE, TILE)] = (total / count).astype(bf)
        spread(c)

    def relay(c):
        at = pl.ds(COL[c], WIDE)
        arrive(everyone.at[pl.ds(0, NX - 1), :, at], x_rs.at[c])
        for dx in (1, 3, 2):
            block = everyone.at[lax.rem(d + 2 * dx, 2 * NX), :, at]
            send(block, block, S, s_rs.at[c], sibling)

    def gathered(c):
        arrive(everyone.at[pl.ds(0, NX), :, pl.ds(COL[c], WIDE)], s_rs.at[c])

    band = NY * rows

    def bands(c):
        return range(COL[c] // band, (COL[c] + WIDE) // band)

    def gradient(c):
        cot_all = cot[...].reshape(groups * spn, columns)
        for b in bands(c):
            lhs = everyone[:, :, pl.ds(b * band, band)].reshape(groups * spn, band)
            out = lax.dot_general(
                lhs, cot_all, (((0,), (0,)), ((), ())), preferred_element_type=f32
            ).astype(bf)
            for q in range(NY):
                part[b, q] = pack(out[q * rows : (q + 1) * rows])
            for j in range(1, NY):
                send(
                    part.at[b, lax.rem(y + j, NY)], part_in.at[b, NY - j],
                    GY, gy_rs.at[b], at_y(j),
                )

    def to_owner(b):
        send(summed.at[b], summed_in.at[z], GZ, gz_rs.at[0], (d, b * NY + y))

    def gather_band(b):
        arrive(part_in.at[b, pl.ds(1, NY - 1)], gy_rs.at[b])
        total = part[b, y].astype(f32)
        for j in range(1, NY):
            total = total + part_in[b, j].astype(f32)

        @pl.when(z == b)
        def _():
            own_sum[...] = total

        @pl.when(z != b)
        def _():
            summed[b] = total.astype(bf)
            to_owner(b)

    def project(c, first=False, final=False):
        def body(n, carry):
            g = pl.ds(2 * n, 2)
            out = lax.dot_general(
                everyone[g, :, pl.ds(COL[c], WIDE)].reshape(2 * spn, WIDE),
                w_proj[:, pl.ds(COL[c], WIDE)], last, preferred_element_type=f32,
            ).reshape(2, spn, columns)
            if not first:
                out = out + acc[g]
            if final:
                student[g] = out.astype(bf)
            else:
                acc[g] = out
            return carry

        lax.fori_loop(0, groups // 2, body, 0)

    for h in (0, 1):
        dispatch(0, h)
    arrive(meta.at[pl.ds(1, NZ - 1)], meta_rs.at[0])
    for p in (1, 2, 3):
        a, b = 2 * p - 1, 2 * p
        for h in (0, 1):
            z_recv(a, h)
            if p < 3:
                z_send(zbuf.at[a], a + 2, h, 1)
            elif h == 0:
                z_send(zbuf.at[a], 7, h, 1)
            z_recv(b, h)
            if p < 3:
                z_send(zbuf.at[b], b + 2, h, -1)
            elif h == 1:
                z_send(zbuf.at[b], 7, h, -1)
            dispatch(a, h)
            if p == 1:
                dispatch(b, h)
        if p == 1:
            for j in range(1, NY):
                send(meta, meta_y.at[NY - j], MY, my_rs.at[0], at_y(j))
            for load in loads:
                load.wait()
            ffn(0)
        if p == 2:
            ffn(1)
        if p == 3:
            ffn(2)
    for h in (0, 1):
        z_recv(7, h)
        dispatch(7, h)
    for i in (6, 4):
        for h in (0, 1):
            dispatch(i, h)
    arrive(meta_y.at[pl.ds(1, NY - 1)], my_rs.at[0])
    for i in range(NZ):
        mixing(i)
    for i in (3, 5, 7):
        ffn(i)
    pass_on(ZA, 4)
    pass_on(ZB, 4)
    ffn(6)
    for i in (5, 7, 6):
        give_back(YA, i)
    pass_on(ZA, 3)
    pass_on(ZB, 3)
    ffn(4)
    give_back(YA, 3)
    give_back(YA, 4)
    pass_on(ZA, 2)
    for i in (1, 2, 0):
        give_back(YA, i)
    pass_on(YA, 4)
    pass_on(ZB, 2)
    pass_on(YA, 3)
    pass_on(ZA, 1)
    for i in (5, 7, 6):
        give_back(YB, i)
    pass_on(YA, 2)
    pass_on(ZB, 1)
    pass_on(YA, 1)
    finish_z(ZA)
    for i in (3, 4, 1, 2, 0):
        give_back(YB, i)
    finish_y(YA)
    pass_on(YB, 4)
    pass_on(YB, 3)
    finish_z_pooled(ZA)
    finish_z(ZB)
    pass_on(YB, 2)
    relay(YA)
    relay(ZA)
    pass_on(YB, 1)
    gathered(YA)
    gradient(YA)
    finish_z_pooled(ZB)
    gathered(ZA)
    gradient(ZA)
    finish_y(YB)
    project(YA, first=True)
    project(ZA)
    for b in list(bands(YA)) + list(bands(ZA)):
        gather_band(b)
    relay(ZB)
    relay(YB)
    gathered(ZB)
    gradient(ZB)
    gathered(YB)
    gradient(YB)
    project(ZB)
    project(YB, final=True)
    for b in list(bands(ZB)) + list(bands(YB)):
        gather_band(b)
    arrive(summed_in.at[pl.ds(0, NZ - 1)], gz_rs.at[0])
    total = own_sum[...]
    for dz in range(1, NZ):
        src = lax.rem(z + dz, NZ)
        total = total + summed_in[src].astype(f32)
    grad[...] = unpack(total, rows)
    sent(meta_out.at[pl.ds(1, NZ - 1)], META)
    sent(meta_y.at[pl.ds(1, NY - 1)], MY)
    sent(zbuf.at[pl.ds(1, NZ - 1)], Z)
    sent(sbuf, Y)
    sent(bbuf.at[:, pl.ds(CAP, (NY - 1) * CAP)], B)
    for kind, buf in ((CZ, msg_z), (CY, msg_y)):
        sent(buf.at[:, :, :, pl.ds(0, 7 * buf.shape[3] // 8)], kind)
    sent(fin_out.at[pl.ds(1, NY - 1)], F)
    sent(everyone.at[pl.ds(0, NX - 1)], X)
    sent(everyone.at[pl.ds(0, NX)], S)
    sent(part.at[:, pl.ds(1, NY - 1)], GY)
    sent(summed.at[pl.ds(1, NZ - 1)], GZ)


def hand_on(student_in, grad_in, student, grad):
    student[...] = student_in[...]
    grad[...] = grad_in[...]


def local(tokens, expert_ids, gate_weights, span_ids, w_gate, w_up, w_down, w_proj, cotangent):
    tok, width = tokens.shape
    ff = w_gate.shape[2]
    topk = expert_ids.shape[1]
    spn = tok // 2
    groups, _, columns = cotangent.shape
    rows = width // (NZ * NY)
    packed = (rows * columns // 128, 128)
    bf, f32 = jnp.bfloat16, jnp.float32
    vmem = pl.BlockSpec(memory_space=pltpu.VMEM)
    hbm = pl.BlockSpec(memory_space=pl.ANY)
    scratch, dma = pltpu.VMEM, pltpu.SemaphoreType.DMA
    results = pl.pallas_call(
        kernel,
        out_shape=(
            jax.ShapeDtypeStruct((groups, spn, columns), bf),
            jax.ShapeDtypeStruct((rows, columns), f32),
        ),
        in_specs=[vmem, hbm, vmem, vmem, hbm, hbm, hbm, hbm, hbm],
        out_specs=(vmem, vmem),
        scratch_shapes=[
            scratch((topk, tok), jnp.int32),
            scratch((width, ff), bf),
            scratch((width, ff), bf),
            scratch((ff, width), bf),
            scratch((columns, width), bf),
            scratch((groups, spn, columns), bf),
            scratch((NZ * NY, tok), f32),
            scratch((NZ * NY, tok), f32),
            scratch((NZ, 16, tok), f32),
            scratch((NZ, 16, tok), bf),
            scratch((NZ, 16, tok), bf),
            scratch((NY, NZ, 16, tok), bf),
            scratch((NZ, spn, NY * CAP), bf),
            scratch((NZ, NY * spn, NY * CAP), bf),
            scratch((NZ, tok, width), bf),
            scratch((NZ, (NY - 1) * CAP, width), bf),
            scratch((NZ, NY * CAP, width), bf),
            scratch((NY * CAP, ff), bf),
            scratch((NZ, NY * CAP, width), bf),
            scratch((NZ, NY * CAP, 2 * WIDE), bf),
            scratch((2, NZ // 2, spn, 2 * WIDE), bf),
            scratch((2, NZ // 2, spn, 2 * WIDE), bf),
            scratch((2, NZ // 2, NY * spn, 2 * WIDE), bf),
            scratch((2, NZ // 2, NY * spn, 2 * WIDE), bf),
            scratch((NY, spn, 2 * WIDE), bf),
            scratch((NY, spn, 2 * WIDE), bf),
            scratch((groups, spn, width), bf),
            scratch((groups, spn, columns), f32),
            scratch((NZ, NY) + packed, bf),
            scratch((NZ, NY) + packed, bf),
            scratch((NZ,) + packed, bf),
            scratch((NZ,) + packed, bf),
            scratch(packed, f32),
            dma((6,)),
            dma((12,)),
            dma((1,)),
            dma((1,)),
            dma((NZ, 2)),
            dma((NZ,)),
            dma((2, NZ)),
            dma((4, 2, NZ // 2)),
            dma((2,)),
            dma((4,)),
            dma((4,)),
            dma((NZ,)),
            dma((1,)),
        ],
        compiler_params=pltpu.CompilerParams(
            collective_id=0, has_side_effects=True, vmem_limit_bytes=62 * 2**20
        ),
    )(
        tokens, expert_ids.T, gate_weights.T, span_ids, w_gate, w_up, w_down, w_proj.T, cotangent
    )
    return pl.pallas_call(
        hand_on,
        out_shape=[jax.ShapeDtypeStruct(r.shape, r.dtype) for r in results],
        in_specs=[vmem] * 2,
        out_specs=[vmem] * 2,
    )(*results)


def solution(mesh):
    placed = (
        P(("dp", "expert"), None),
        P("dp", None),
        P(("dp", "expert"), None),
        P(None, "expert"),
        P("expert", None, None),
        P("expert", None, None),
        P("expert", None, None),
        P(None, "dp"),
        P(None, "expert", "dp"),
    )
    return jax.shard_map(
        local,
        mesh=mesh,
        in_specs=placed,
        out_specs=(P(None, "expert", "dp"), P("expert", "dp")),
        check_vma=False,
    )
```

```python
import jax
import jax.numpy as jnp
from jax import lax
from jax.experimental import pallas as pl
from jax.experimental.pallas import tpu as pltpu
from jax.sharding import PartitionSpec as P

MESH = pl.DeviceIdType.MESH
NX, NZ, NY = 4, 8, 4
CAP = 48
DELTA = (0, -1, 1, -2, 2, -3, 3, 4)
PAIR = (0, 2, 1, 4, 3, 6, 5, 7)
HOP = {4: (7, 7), 3: (6, 5), 2: (4, 3), 1: (2, 1)}
TILE = 256
ZA, YA, ZB, YB = 0, 1, 2, 3
ON_Z = (True, False, True, False)
WIDE = (512, 512, 512, 512)
COL = (0, WIDE[0], WIDE[0] + WIDE[1], sum(WIDE[:3]))
OFF = (0, 0, WIDE[0], WIDE[1])
Z_WIDE, Y_WIDE = WIDE[0] + WIDE[2], WIDE[1] + WIDE[3]
BAND = (0, 4, 2, 6, 1, 5, 3, 7)
META, MY, Z, Y, B, CZ, CY, F, X, S, GY, GZ = range(12)


def place():
    d = lax.axis_index("dp")
    e = lax.axis_index("expert")
    return d, e // NY, lax.rem(e, NY)


def pack(g):
    half = g.shape[0] // 2
    tail = jnp.concatenate([g[:half, 256:], g[half:, 256:]], axis=1)
    return jnp.concatenate([g[:, :128], g[:, 128:256], tail], axis=0)


def unpack(p, rows):
    tail = p[2 * rows :]
    tail = jnp.concatenate([tail[:, :64], tail[:, 64:]], axis=0)
    return jnp.concatenate([p[:rows], p[rows : 2 * rows], tail], axis=1)


def kernel(
    tokens, ids_hbm, gates, spans, wg_hbm, wu_hbm, wd_hbm, proj_hbm, cot_hbm, student, grad,
    ids, wg, wu, wd, w_proj, cot, slot_t, gate_t, lines, meta_out, meta, meta_y, mix_y, mix_z,
    zbuf, sbuf, xbuf, hid, rbuf, bbuf, msg_y, got_y, msg_z, got_z, fin_out, fin_in,
    everyone, acc, part, part_in, summed, summed_in, own_sum,
    load_sem, send_sem, meta_rs, my_rs, z_rs, y_rs, b_rs, c_rs, f_rs, x_rs, s_rs, gy_rs, gz_rs,
):
    d, z, y = place()
    e = z * NY + y
    x, core = d // 2, lax.rem(d, 2)
    me = (d, e)
    sibling = (2 * x + 1 - core, e)
    tok, width = tokens.shape
    ff = wg.shape[1]
    groups, spn, columns = cot.shape
    rows = grad.shape[0]
    f32, bf = jnp.float32, jnp.bfloat16

    def at_z(dz):
        return (d, lax.rem(z + NZ + dz, NZ) * NY + y)

    def at_y(dy):
        return (d, z * NY + lax.rem(y + NY + dy, NY))

    def at_x(dx):
        return (lax.rem(d + 2 * NX + 2 * dx, 2 * NX), e)

    barrier = pltpu.get_barrier_semaphore()
    peers = [at_z(dz) for dz in DELTA[1:]]
    peers += [at_y(dy) for dy in range(1, NY)]
    peers += [at_x(dx) for dx in range(1, NX)] + [sibling]
    for peer in peers:
        pl.semaphore_signal(barrier, inc=1, device_id=peer, device_id_type=MESH)
    ids_copy = pltpu.make_async_copy(
        ids_hbm.at[:, pl.ds(pl.multiple_of(e * tok, tok), tok)], ids, load_sem.at[0]
    )
    ids_copy.start()
    loads = [
        pltpu.make_async_copy(src, dst, load_sem.at[n + 1])
        for n, (src, dst) in enumerate(
            (
                (wg_hbm.at[0], wg),
                (wu_hbm.at[0], wu),
                (cot_hbm, cot),
                (wd_hbm.at[0], wd),
                (proj_hbm, w_proj),
            )
        )
    ]
    for load in loads[:3]:
        load.start()
    wide_band = width // NZ
    for n, (src, dst) in ((4, (wd_hbm.at[0], wd)), (5, (proj_hbm, w_proj))):
        for p in range(NZ):
            there = pl.ds(BAND[p] * wide_band, wide_band)
            here = pl.ds(p * wide_band, wide_band)
            pltpu.make_async_copy(src.at[:, there], dst.at[:, here], load_sem.at[n]).start()

    def remote(src, dst, ss, rs, dev):
        return pltpu.make_async_remote_copy(
            src_ref=src, dst_ref=dst, send_sem=ss, recv_sem=rs, device_id=dev, device_id_type=MESH
        )

    def send(src, dst, kind, rs, dev):
        remote(src, dst, send_sem.at[kind], rs, dev).start()

    def sent(src, kind):
        remote(src, src, send_sem.at[kind], load_sem.at[0], me).wait_send()

    def arrive(dst, rs):
        remote(dst, dst, send_sem.at[0], rs, me).wait_recv()

    half = [pl.ds(h * (width // 2), width // 2) for h in (0, 1)]

    def z_send(src, s, h, dz):
        send(src.at[:, half[h]], zbuf.at[s, :, half[h]], Z, z_rs.at[s, h], at_z(dz))

    def z_recv(s, h):
        arrive(zbuf.at[s, :, half[h]], z_rs.at[s, h])

    ids_copy.wait()
    experts = NZ * NY
    number = lax.broadcasted_iota(jnp.int32, (experts, tok), 0)
    taken = jnp.zeros((experts, tok), f32)
    weight = jnp.zeros((experts, tok), f32)
    for k in range(ids.shape[0]):
        named = ids[k : k + 1, :] == number
        taken = taken + jnp.where(named, 1.0, 0.0)
        weight = weight + jnp.where(named, gates[k : k + 1, :], 0.0)
    row = lax.broadcasted_iota(jnp.int32, (tok, tok), 0)
    col = lax.broadcasted_iota(jnp.int32, (tok, tok), 1)
    earlier = jnp.where(row < col, 1.0, 0.0).astype(bf)
    before = jnp.dot(taken.astype(bf), earlier, preferred_element_type=f32)
    slot_t[...] = jnp.where(taken > 0.0, before, -1.0)
    gate_t[...] = weight
    own_span = spans[pl.ds(d, 1), :].astype(f32)
    lines[...] = jnp.zeros(lines.shape, f32)
    for i in range(NZ):
        there = lax.rem(z + NZ + DELTA[i], NZ) * NY
        for j in range(NY):
            line = there + lax.rem(y + j, NY)
            lines[i, j : j + 1, :] = slot_t[pl.ds(line, 1), :]
            lines[i, NY + j : NY + j + 1, :] = gate_t[pl.ds(line, 1), :]
        lines[i, 2 * NY : 2 * NY + 1, :] = own_span
        if i == 0:
            meta[0] = lines[0].astype(bf)
        else:
            meta_out[i] = lines[i].astype(bf)
    slots = lax.broadcasted_iota(jnp.int32, (CAP, tok), 0).astype(f32)
    span_rows = lax.broadcasted_iota(jnp.int32, (spn, tok), 0).astype(f32)
    last = (((1,), (1,)), ((), ()))

    def onehot(slab, j):
        return jnp.where(slab[j : j + 1, :] == slots, 1.0, 0.0).astype(bf)

    def select(i, h):
        block = tokens if i == 0 else zbuf.at[i]
        slab = meta[i].astype(f32)
        pick = jnp.concatenate([onehot(slab, j) for j in range(NY)], axis=0)

        def body(n, carry):
            at = pl.ds(pl.multiple_of(h * (width // 2) + n * 512, 512), 512)
            out = jnp.dot(pick, block[:, at], preferred_element_type=f32).astype(bf)
            xbuf[i, 0:CAP, at] = out[0:CAP]
            sbuf[i, :, at] = out[CAP:]
            return carry

        lax.fori_loop(0, width // 1024, body, 0)

    def dispatch(i, h):
        if i > 0:
            select(i, h)
        for j in range(1, NY):
            back = NY - j
            send(
                sbuf.at[i, pl.ds((j - 1) * CAP, CAP), half[h]],
                xbuf.at[i, pl.ds(back * CAP, CAP), half[h]],
                Y, y_rs.at[i], at_y(j),
            )

    def ffn(i):
        arrive(xbuf.at[i, pl.ds(CAP, (NY - 1) * CAP)], y_rs.at[i])

        def up(n, carry):
            at = pl.ds(pl.multiple_of(n * TILE, TILE), TILE)
            rows_in = xbuf[i]
            g = jnp.dot(rows_in, wg[:, at], preferred_element_type=f32)
            u = jnp.dot(rows_in, wu[:, at], preferred_element_type=f32)
            hid[:, at] = (g / (1.0 + jnp.exp(-g)) * u).astype(bf)
            return carry

        lax.fori_loop(0, ff // TILE, up, 0)
        for c in range(4):

            def down(n, carry):
                at = pl.ds(pl.multiple_of(COL[c] + n * TILE, TILE), TILE)
                out = jnp.dot(hid[...], wd[:, at], preferred_element_type=f32).astype(bf)
                rbuf[i, :, at] = out
                if not ON_Z[c]:
                    own = pl.ds(pl.multiple_of(OFF[c] + n * TILE, TILE), TILE)
                    bbuf[i, 0:CAP, own] = out[0:CAP]
                return carry

            lax.fori_loop(0, WIDE[c] // TILE, down, 0)

    def pooling(slab, j):
        gate = slab[NY + j : NY + j + 1, :]
        share = jnp.where(slab[2 * NY : 2 * NY + 1, :] == span_rows, gate, 0.0).astype(bf)
        out = lax.dot_general(share, onehot(slab, j), last, preferred_element_type=f32)
        return out.astype(bf)

    def mixing(i):
        own = meta[i].astype(f32)
        mix_y[i] = jnp.concatenate([pooling(own, j) for j in range(NY)], axis=1)
        for j in range(NY):
            slab = own if j == 0 else meta_y[j, i].astype(f32)
            mine = pooling(slab, (NY - j) % NY)
            pieces = [mine if q == j else jnp.zeros((spn, CAP), bf) for q in range(NY)]
            mix_z[i, j * spn : (j + 1) * spn] = jnp.concatenate(pieces, axis=1)

    def give_back(c, i):
        src = pl.ds(COL[c], WIDE[c])
        dst = pl.ds(OFF[c], WIDE[c])
        for j in range(1, NY):
            back = NY - j
            send(
                rbuf.at[i, pl.ds(j * CAP, CAP), src], bbuf.at[i, pl.ds(back * CAP, CAP), dst],
                B, b_rs.at[c // 2, i], at_y(j),
            )

    def returned(c, i):
        arrive(
            bbuf.at[i, pl.ds(CAP, (NY - 1) * CAP), pl.ds(OFF[c], WIDE[c])], b_rs.at[c // 2, i]
        )

    def term(c, i, n, part_rows=None):
        mix = mix_z.at[i] if ON_Z[c] else mix_y.at[i]
        mix = mix[...] if part_rows is None else mix[part_rows, :]
        if ON_Z[c]:
            block = rbuf[i, :, pl.ds(COL[c] + n * TILE, TILE)]
        else:
            block = bbuf[i, :, pl.ds(OFF[c] + n * TILE, TILE)]
        return jnp.dot(mix, block, preferred_element_type=f32)

    def chain_part(buf, c, way, hop):
        at = pl.ds(OFF[c], WIDE[c])
        total = buf.shape[2]
        if hop == NZ // 2:
            return buf.at[way, hop - 1, pl.ds(way * (total // 2), total // 2), at]
        return buf.at[way, hop - 1, :, at]

    def chain_recv(c, way, hop):
        got = got_z if ON_Z[c] else got_y
        arrive(chain_part(got, c, way, hop), c_rs.at[c, way, hop - 1])

    def pass_on(c, hop):
        msg, got = (msg_z, got_z) if ON_Z[c] else (msg_y, got_y)
        half = msg.shape[2] // 2
        for way in (0, 1):
            i = HOP[hop][way]
            if not ON_Z[c] and not (hop == 4 and way == 1):
                returned(c, i)
            if hop < 4:
                chain_recv(c, way, hop + 1)
            side, other = pl.ds(way * half, half), pl.ds((1 - way) * half, half)
            for n in range(WIDE[c] // TILE):
                at = pl.ds(OFF[c] + n * TILE, TILE)
                if hop == 4:
                    msg[way, 3, side, at] = term(c, i, n, side).astype(bf)
                elif hop == 3:
                    came = got[way, 3, side, at].astype(f32)
                    msg[way, 2, side, at] = (term(c, i, n, side) + came).astype(bf)
                    msg[way, 2, other, at] = term(c, i, n, other).astype(bf)
                else:
                    came = got[way, hop, :, at].astype(f32)
                    msg[way, hop - 1, :, at] = (term(c, i, n) + came).astype(bf)
            send(
                chain_part(msg, c, way, hop), chain_part(got, c, way, hop),
                CZ if ON_Z[c] else CY, c_rs.at[c, way, hop - 1], at_z(1 - 2 * way),
            )

    count = jnp.sum(jnp.where(own_span == span_rows, 1.0, 0.0), axis=1, keepdims=True)

    def spread(c):
        mine = everyone.at[d, :, pl.ds(COL[c], WIDE[c])]
        for dx in (1, 3, 2):
            send(mine, mine, X, x_rs.at[c], at_x(dx))
        send(mine, mine, S, s_rs.at[c], sibling)

    def finish_z(c):
        chain_recv(c, 0, 1)
        chain_recv(c, 1, 1)
        for n in range(WIDE[c] // TILE):
            at = pl.ds(OFF[c] + n * TILE, TILE)
            total = term(c, 0, n) + got_z[0, 0, :, at].astype(f32) + got_z[1, 0, :, at].astype(f32)
            fin_out[:, :, at] = total.astype(bf).reshape(NY, spn, TILE)
        at = pl.ds(OFF[c], WIDE[c])
        for j in range(1, NY):
            send(
                fin_out.at[j, :, at], fin_in.at[NY - j, :, at],
                F, f_rs.at[c // 2], at_y(j),
            )

    def finish_z_pooled(c):
        at = pl.ds(OFF[c], WIDE[c])
        total = fin_out[0, :, at].astype(f32)
        arrive(fin_in.at[pl.ds(1, NY - 1), :, at], f_rs.at[c // 2])
        for j in range(1, NY):
            total = total + fin_in[j, :, at].astype(f32)
        everyone[d, :, pl.ds(COL[c], WIDE[c])] = (total / count).astype(bf)
        spread(c)

    def finish_y(c):
        returned(c, 0)
        chain_recv(c, 0, 1)
        chain_recv(c, 1, 1)
        for n in range(WIDE[c] // TILE):
            at = pl.ds(OFF[c] + n * TILE, TILE)
            total = term(c, 0, n) + got_y[0, 0, :, at].astype(f32) + got_y[1, 0, :, at].astype(f32)
            everyone[d, :, pl.ds(COL[c] + n * TILE, TILE)] = (total / count).astype(bf)
        spread(c)

    def relay(c):
        at = pl.ds(COL[c], WIDE[c])
        arrive(everyone.at[pl.ds(0, NX - 1), :, at], x_rs.at[c])
        for dx in (1, 3, 2):
            block = everyone.at[lax.rem(d + 2 * dx, 2 * NX), :, at]
            send(block, block, S, s_rs.at[c], sibling)

    def gathered(c):
        arrive(everyone.at[pl.ds(0, NX), :, pl.ds(COL[c], WIDE[c])], s_rs.at[c])

    band = NY * rows

    def places(c):
        return range(COL[c] // band, (COL[c] + WIDE[c]) // band)

    def bands(c):
        return [BAND[p] for p in places(c)]

    def gradient(c):
        cot_all = cot[...].reshape(groups * spn, columns)
        for p in places(c):
            b = BAND[p]
            lhs = everyone[:, :, pl.ds(p * band, band)].reshape(groups * spn, band)
            out = lax.dot_general(
                lhs, cot_all, (((0,), (0,)), ((), ())), preferred_element_type=f32
            ).astype(bf)
            for q in range(NY):
                part[b, q] = pack(out[q * rows : (q + 1) * rows])
            for j in range(1, NY):
                send(
                    part.at[b, lax.rem(y + j, NY)], part_in.at[b, NY - j],
                    GY, gy_rs.at[b], at_y(j),
                )

    def to_owner(b):
        send(summed.at[b], summed_in.at[z], GZ, gz_rs.at[0], (d, b * NY + y))

    def gather_band(b):
        arrive(part_in.at[b, pl.ds(1, NY - 1)], gy_rs.at[b])
        total = part[b, y].astype(f32)
        for j in range(1, NY):
            total = total + part_in[b, j].astype(f32)

        @pl.when(z == b)
        def _():
            own_sum[...] = total

        @pl.when(z != b)
        def _():
            summed[b] = total.astype(bf)
            to_owner(b)

    def project(c, first=False, final=False):
        def body(n, carry):
            g = pl.ds(2 * n, 2)
            out = lax.dot_general(
                everyone[g, :, pl.ds(COL[c], WIDE[c])].reshape(2 * spn, WIDE[c]),
                w_proj[:, pl.ds(COL[c], WIDE[c])], last, preferred_element_type=f32,
            ).reshape(2, spn, columns)
            if not first:
                out = out + acc[g]
            if final:
                student[g] = out.astype(bf)
            else:
                acc[g] = out
            return carry

        lax.fori_loop(0, groups // 2, body, 0)

    for h in (0, 1):
        select(0, h)
    pl.semaphore_wait(barrier, len(peers))
    for i in range(1, NZ):
        send(meta_out.at[i], meta.at[PAIR[i]], META, meta_rs.at[0], at_z(DELTA[i]))
    for h in (0, 1):
        z_send(tokens, 1, h, 1)
        z_send(tokens, 2, h, -1)
    for h in (0, 1):
        dispatch(0, h)
    arrive(meta.at[pl.ds(1, NZ - 1)], meta_rs.at[0])
    for p in (1, 2, 3):
        a, b = 2 * p - 1, 2 * p
        for h in (0, 1):
            z_recv(a, h)
            if p < 3:
                z_send(zbuf.at[a], a + 2, h, 1)
            elif h == 0:
                z_send(zbuf.at[a], 7, h, 1)
            z_recv(b, h)
            if p < 3:
                z_send(zbuf.at[b], b + 2, h, -1)
            elif h == 1:
                z_send(zbuf.at[b], 7, h, -1)
            dispatch(a, h)
            if p == 1:
                dispatch(b, h)
        if p == 1:
            for j in range(1, NY):
                send(meta, meta_y.at[NY - j], MY, my_rs.at[0], at_y(j))
            for load in loads:
                load.wait()
            ffn(0)
        if p == 2:
            ffn(1)
        if p == 3:
            ffn(2)
    for h in (0, 1):
        z_recv(7, h)
        dispatch(7, h)
    for i in (6, 4):
        for h in (0, 1):
            dispatch(i, h)
    arrive(meta_y.at[pl.ds(1, NY - 1)], my_rs.at[0])
    for i in range(NZ):
        mixing(i)
    for i in (3, 5, 7):
        ffn(i)
    pass_on(ZA, 4)
    pass_on(ZB, 4)
    ffn(6)
    give_back(YA, 5)
    give_back(YA, 7)
    give_back(YA, 6)
    pass_on(ZA, 3)
    pass_on(ZB, 3)
    ffn(4)
    give_back(YA, 3)
    give_back(YA, 4)
    pass_on(ZA, 2)
    give_back(YA, 1)
    give_back(YA, 2)
    give_back(YA, 0)
    pass_on(YA, 4)
    pass_on(ZB, 2)
    give_back(YB, 5)
    give_back(YB, 7)
    give_back(YB, 6)
    pass_on(YA, 3)
    pass_on(ZA, 1)
    give_back(YB, 3)
    give_back(YB, 4)
    pass_on(YA, 2)
    pass_on(ZB, 1)
    give_back(YB, 1)
    give_back(YB, 2)
    give_back(YB, 0)
    pass_on(YA, 1)
    finish_z(ZA)
    finish_y(YA)
    pass_on(YB, 4)
    pass_on(YB, 3)
    finish_z_pooled(ZA)
    finish_z(ZB)
    pass_on(YB, 2)
    relay(YA)
    relay(ZA)
    pass_on(YB, 1)
    gathered(YA)
    gradient(YA)
    finish_z_pooled(ZB)
    finish_y(YB)
    gathered(ZA)
    gradient(ZA)
    for b in bands(YA):
        gather_band(b)
    relay(ZB)
    relay(YB)
    gathered(ZB)
    gradient(ZB)
    gathered(YB)
    gradient(YB)
    for b in bands(ZA):
        gather_band(b)
    project(YA, first=True)
    project(ZA)
    for b in bands(ZB):
        gather_band(b)
    for b in bands(YB):
        gather_band(b)
    project(ZB)
    project(YB, final=True)
    arrive(summed_in.at[pl.ds(0, NZ - 1)], gz_rs.at[0])
    total = own_sum[...]
    for dz in range(1, NZ):
        src = lax.rem(z + dz, NZ)
        total = total + summed_in[src].astype(f32)
    grad[...] = unpack(total, rows)
    sent(meta_out.at[pl.ds(1, NZ - 1)], META)
    sent(meta_y.at[pl.ds(1, NY - 1)], MY)
    sent(zbuf.at[pl.ds(1, NZ - 1)], Z)
    sent(sbuf, Y)
    sent(bbuf.at[:, pl.ds(CAP, (NY - 1) * CAP)], B)
    sent(msg_z.at[:, :, pl.ds(0, 7 * NY * spn // 8)], CZ)
    sent(zbuf.at[pl.ds(0, 7), pl.ds(0, spn), pl.ds(0, Y_WIDE)], CY)
    sent(fin_out.at[pl.ds(1, NY - 1)], F)
    sent(everyone.at[pl.ds(0, NX - 1)], X)
    sent(everyone.at[pl.ds(0, NX)], S)
    sent(part.at[:, pl.ds(1, NY - 1)], GY)
    sent(summed.at[pl.ds(1, NZ - 1)], GZ)


def hand_on(student_in, grad_in, student, grad):
    student[...] = student_in[...]
    grad[...] = grad_in[...]


def local(tokens, expert_ids, gate_weights, span_ids, w_gate, w_up, w_down, w_proj, cotangent):
    tok, width = tokens.shape
    ff = w_gate.shape[2]
    topk = expert_ids.shape[1]
    spn = tok // 2
    groups, _, columns = cotangent.shape
    rows = width // (NZ * NY)
    packed = (rows * columns // 128, 128)
    bf, f32 = jnp.bfloat16, jnp.float32
    vmem = pl.BlockSpec(memory_space=pltpu.VMEM)
    hbm = pl.BlockSpec(memory_space=pl.ANY)
    scratch, dma = pltpu.VMEM, pltpu.SemaphoreType.DMA
    results = pl.pallas_call(
        kernel,
        out_shape=(
            jax.ShapeDtypeStruct((groups, spn, columns), bf),
            jax.ShapeDtypeStruct((rows, columns), f32),
        ),
        in_specs=[vmem, hbm, vmem, vmem, hbm, hbm, hbm, hbm, hbm],
        out_specs=(vmem, vmem),
        scratch_shapes=[
            scratch((topk, tok), jnp.int32),
            scratch((width, ff), bf),
            scratch((width, ff), bf),
            scratch((ff, width), bf),
            scratch((columns, width), bf),
            scratch((groups, spn, columns), bf),
            scratch((NZ * NY, tok), f32),
            scratch((NZ * NY, tok), f32),
            scratch((NZ, 16, tok), f32),
            scratch((NZ, 16, tok), bf),
            scratch((NZ, 16, tok), bf),
            scratch((NY, NZ, 16, tok), bf),
            scratch((NZ, spn, NY * CAP), bf),
            scratch((NZ, NY * spn, NY * CAP), bf),
            scratch((NZ, tok, width), bf),
            scratch((NZ, (NY - 1) * CAP, width), bf),
            scratch((NZ, NY * CAP, width), bf),
            scratch((NY * CAP, ff), bf),
            scratch((NZ, NY * CAP, width), bf),
            scratch((NZ, NY * CAP, Y_WIDE), bf),
            scratch((2, NZ // 2, spn, Y_WIDE), bf),
            scratch((2, NZ // 2, spn, Y_WIDE), bf),
            scratch((2, NZ // 2, NY * spn, Z_WIDE), bf),
            scratch((2, NZ // 2, NY * spn, Z_WIDE), bf),
            scratch((NY, spn, Z_WIDE), bf),
            scratch((NY, spn, Z_WIDE), bf),
            scratch((groups, spn, width), bf),
            scratch((groups, spn, columns), f32),
            scratch((NZ, NY) + packed, bf),
            scratch((NZ, NY) + packed, bf),
            scratch((NZ,) + packed, bf),
            scratch((NZ,) + packed, bf),
            scratch(packed, f32),
            dma((6,)),
            dma((12,)),
            dma((1,)),
            dma((1,)),
            dma((NZ, 2)),
            dma((NZ,)),
            dma((2, NZ)),
            dma((4, 2, NZ // 2)),
            dma((2,)),
            dma((4,)),
            dma((4,)),
            dma((NZ,)),
            dma((1,)),
        ],
        compiler_params=pltpu.CompilerParams(
            collective_id=0, has_side_effects=True, vmem_limit_bytes=62 * 2**20
        ),
    )(
        tokens, expert_ids.T, gate_weights.T, span_ids, w_gate, w_up, w_down, w_proj.T, cotangent
    )
    return pl.pallas_call(
        hand_on,
        out_shape=[jax.ShapeDtypeStruct(r.shape, r.dtype) for r in results],
        in_specs=[vmem] * 2,
        out_specs=[vmem] * 2,
    )(*results)


def solution(mesh):
    placed = (
        P(("dp", "expert"), None),
        P("dp", None),
        P(("dp", "expert"), None),
        P(None, "expert"),
        P("expert", None, None),
        P("expert", None, None),
        P("expert", None, None),
        P(None, "dp"),
        P(None, "expert", "dp"),
    )
    return jax.shard_map(
        local,
        mesh=mesh,
        in_specs=placed,
        out_specs=(P(None, "expert", "dp"), P("expert", "dp")),
        check_vma=False,
    )
```

```python
import jax
import jax.numpy as jnp
from jax import lax
from jax.experimental import pallas as pl
from jax.experimental.pallas import tpu as pltpu
from jax.sharding import PartitionSpec as P

MESH = pl.DeviceIdType.MESH
NX, NZ, NY = 4, 8, 4
CAP = 48
DELTA = (0, -1, 1, -2, 2, -3, 3, 4)
PAIR = (0, 2, 1, 4, 3, 6, 5, 7)
HOP = {4: (7, 7), 3: (6, 5), 2: (4, 3), 1: (2, 1)}
TILE = 256
ZA, YA, ZB, YB = 0, 1, 2, 3
ON_Z = (True, False, True, False)
WIDE = (512, 512, 512, 512)
COL = (0, WIDE[0], WIDE[0] + WIDE[1], sum(WIDE[:3]))
OFF = (0, 0, WIDE[0], WIDE[1])
Z_WIDE, Y_WIDE = WIDE[0] + WIDE[2], WIDE[1] + WIDE[3]
BAND = (0, 4, 2, 6, 1, 5, 3, 7)
META, MY, Z, Y, B, CZ, CY, F, X, S, GY, GZ = range(12)


def place():
    d = lax.axis_index("dp")
    e = lax.axis_index("expert")
    return d, e // NY, lax.rem(e, NY)


def pack(g):
    half = g.shape[0] // 2
    tail = jnp.concatenate([g[:half, 256:], g[half:, 256:]], axis=1)
    return jnp.concatenate([g[:, :128], g[:, 128:256], tail], axis=0)


def unpack(p, rows):
    tail = p[2 * rows :]
    tail = jnp.concatenate([tail[:, :64], tail[:, 64:]], axis=0)
    return jnp.concatenate([p[:rows], p[rows : 2 * rows], tail], axis=1)


def kernel(
    tokens, ids_hbm, gates, spans, wg_hbm, wu_hbm, wd_hbm, proj_hbm, cot_hbm, student, grad,
    ids, wg, wu, wd, w_proj, cot, slot_t, gate_t, lines, meta_out, meta, meta_y, mix_y, mix_z,
    zbuf, sbuf, xbuf, hid, rbuf, bbuf, msg_y, got_y, msg_z, got_z, fin_out, fin_in,
    everyone, acc, part, part_in, summed, summed_in, own_sum,
    load_sem, send_sem, meta_rs, my_rs, z_rs, y_rs, b_rs, c_rs, f_rs, x_rs, s_rs, gy_rs, gz_rs,
):
    d, z, y = place()
    e = z * NY + y
    x, core = d // 2, lax.rem(d, 2)
    me = (d, e)
    sibling = (2 * x + 1 - core, e)
    tok, width = tokens.shape
    ff = wg.shape[1]
    groups, spn, columns = cot.shape
    rows = grad.shape[0]
    f32, bf = jnp.float32, jnp.bfloat16

    def at_z(dz):
        return (d, lax.rem(z + NZ + dz, NZ) * NY + y)

    def at_y(dy):
        return (d, z * NY + lax.rem(y + NY + dy, NY))

    def at_x(dx):
        return (lax.rem(d + 2 * NX + 2 * dx, 2 * NX), e)

    barrier = pltpu.get_barrier_semaphore()
    peers = [at_z(dz) for dz in DELTA[1:]]
    peers += [at_y(dy) for dy in range(1, NY)]
    peers += [at_x(dx) for dx in range(1, NX)] + [sibling]
    for peer in peers:
        pl.semaphore_signal(barrier, inc=1, device_id=peer, device_id_type=MESH)
    ids_copy = pltpu.make_async_copy(
        ids_hbm.at[:, pl.ds(pl.multiple_of(e * tok, tok), tok)], ids, load_sem.at[0]
    )
    ids_copy.start()
    loads = [
        pltpu.make_async_copy(src, dst, load_sem.at[n + 1])
        for n, (src, dst) in enumerate(
            (
                (wg_hbm.at[0], wg),
                (wu_hbm.at[0], wu),
                (cot_hbm, cot),
                (wd_hbm.at[0], wd),
                (proj_hbm, w_proj),
            )
        )
    ]
    for load in loads[:3]:
        load.start()
    wide_band = width // NZ
    for n, (src, dst) in ((4, (wd_hbm.at[0], wd)), (5, (proj_hbm, w_proj))):
        for p in range(NZ):
            there = pl.ds(BAND[p] * wide_band, wide_band)
            here = pl.ds(p * wide_band, wide_band)
            pltpu.make_async_copy(src.at[:, there], dst.at[:, here], load_sem.at[n]).start()

    def remote(src, dst, ss, rs, dev):
        return pltpu.make_async_remote_copy(
            src_ref=src, dst_ref=dst, send_sem=ss, recv_sem=rs, device_id=dev, device_id_type=MESH
        )

    def send(src, dst, kind, rs, dev):
        remote(src, dst, send_sem.at[kind], rs, dev).start()

    def sent(src, kind):
        remote(src, src, send_sem.at[kind], load_sem.at[0], me).wait_send()

    def arrive(dst, rs):
        remote(dst, dst, send_sem.at[0], rs, me).wait_recv()

    half = [pl.ds(h * (width // 2), width // 2) for h in (0, 1)]

    def z_send(src, s, h, dz):
        send(src.at[:, half[h]], zbuf.at[s, :, half[h]], Z, z_rs.at[s, h], at_z(dz))

    def z_recv(s, h):
        arrive(zbuf.at[s, :, half[h]], z_rs.at[s, h])

    ids_copy.wait()
    experts = NZ * NY
    number = lax.broadcasted_iota(jnp.int32, (experts, tok), 0)
    taken = jnp.zeros((experts, tok), f32)
    weight = jnp.zeros((experts, tok), f32)
    for k in range(ids.shape[0]):
        named = ids[k : k + 1, :] == number
        taken = taken + jnp.where(named, 1.0, 0.0)
        weight = weight + jnp.where(named, gates[k : k + 1, :], 0.0)
    row = lax.broadcasted_iota(jnp.int32, (tok, tok), 0)
    col = lax.broadcasted_iota(jnp.int32, (tok, tok), 1)
    earlier = jnp.where(row < col, 1.0, 0.0).astype(bf)
    before = jnp.dot(taken.astype(bf), earlier, preferred_element_type=f32)
    slot_t[...] = jnp.where(taken > 0.0, before, -1.0)
    gate_t[...] = weight
    own_span = spans[pl.ds(d, 1), :].astype(f32)
    lines[...] = jnp.zeros(lines.shape, f32)
    for i in range(NZ):
        there = lax.rem(z + NZ + DELTA[i], NZ) * NY
        for j in range(NY):
            line = there + lax.rem(y + j, NY)
            lines[i, j : j + 1, :] = slot_t[pl.ds(line, 1), :]
            lines[i, NY + j : NY + j + 1, :] = gate_t[pl.ds(line, 1), :]
        lines[i, 2 * NY : 2 * NY + 1, :] = own_span
        if i == 0:
            meta[0] = lines[0].astype(bf)
        else:
            meta_out[i] = lines[i].astype(bf)
    slots = lax.broadcasted_iota(jnp.int32, (CAP, tok), 0).astype(f32)
    span_rows = lax.broadcasted_iota(jnp.int32, (spn, tok), 0).astype(f32)
    last = (((1,), (1,)), ((), ()))

    def onehot(slab, j):
        return jnp.where(slab[j : j + 1, :] == slots, 1.0, 0.0).astype(bf)

    def select(i, h):
        block = tokens if i == 0 else zbuf.at[i]
        slab = meta[i].astype(f32)
        pick = jnp.concatenate([onehot(slab, j) for j in range(NY)], axis=0)

        def body(n, carry):
            at = pl.ds(pl.multiple_of(h * (width // 2) + n * 512, 512), 512)
            out = jnp.dot(pick, block[:, at], preferred_element_type=f32).astype(bf)
            xbuf[i, 0:CAP, at] = out[0:CAP]
            sbuf[i, :, at] = out[CAP:]
            return carry

        lax.fori_loop(0, width // 1024, body, 0)

    def dispatch(i, h):
        if i > 0:
            select(i, h)
        for j in range(1, NY):
            back = NY - j
            send(
                sbuf.at[i, pl.ds((j - 1) * CAP, CAP), half[h]],
                xbuf.at[i, pl.ds(back * CAP, CAP), half[h]],
                Y, y_rs.at[i], at_y(j),
            )

    def ffn(i):
        arrive(xbuf.at[i, pl.ds(CAP, (NY - 1) * CAP)], y_rs.at[i])

        def up(n, carry):
            at = pl.ds(pl.multiple_of(n * TILE, TILE), TILE)
            rows_in = xbuf[i]
            g = jnp.dot(rows_in, wg[:, at], preferred_element_type=f32)
            u = jnp.dot(rows_in, wu[:, at], preferred_element_type=f32)
            hid[:, at] = (g / (1.0 + jnp.exp(-g)) * u).astype(bf)
            return carry

        lax.fori_loop(0, ff // TILE, up, 0)
        for c in range(4):

            def down(n, carry):
                at = pl.ds(pl.multiple_of(COL[c] + n * TILE, TILE), TILE)
                out = jnp.dot(hid[...], wd[:, at], preferred_element_type=f32).astype(bf)
                rbuf[i, :, at] = out
                if not ON_Z[c]:
                    own = pl.ds(pl.multiple_of(OFF[c] + n * TILE, TILE), TILE)
                    bbuf[i, 0:CAP, own] = out[0:CAP]
                return carry

            lax.fori_loop(0, WIDE[c] // TILE, down, 0)

    def pooling(slab, j):
        gate = slab[NY + j : NY + j + 1, :]
        share = jnp.where(slab[2 * NY : 2 * NY + 1, :] == span_rows, gate, 0.0).astype(bf)
        out = lax.dot_general(share, onehot(slab, j), last, preferred_element_type=f32)
        return out.astype(bf)

    def mixing(i):
        own = meta[i].astype(f32)
        mix_y[i] = jnp.concatenate([pooling(own, j) for j in range(NY)], axis=1)
        for j in range(NY):
            slab = own if j == 0 else meta_y[j, i].astype(f32)
            mine = pooling(slab, (NY - j) % NY)
            pieces = [mine if q == j else jnp.zeros((spn, CAP), bf) for q in range(NY)]
            mix_z[i, j * spn : (j + 1) * spn] = jnp.concatenate(pieces, axis=1)

    def give_back(c, i):
        src = pl.ds(COL[c], WIDE[c])
        dst = pl.ds(OFF[c], WIDE[c])
        for j in range(1, NY):
            back = NY - j
            send(
                rbuf.at[i, pl.ds(j * CAP, CAP), src], bbuf.at[i, pl.ds(back * CAP, CAP), dst],
                B, b_rs.at[c // 2, i], at_y(j),
            )

    def returned(c, i):
        arrive(
            bbuf.at[i, pl.ds(CAP, (NY - 1) * CAP), pl.ds(OFF[c], WIDE[c])], b_rs.at[c // 2, i]
        )

    def term(c, i, n, part_rows=None):
        mix = mix_z.at[i] if ON_Z[c] else mix_y.at[i]
        mix = mix[...] if part_rows is None else mix[part_rows, :]
        if ON_Z[c]:
            block = rbuf[i, :, pl.ds(COL[c] + n * TILE, TILE)]
        else:
            block = bbuf[i, :, pl.ds(OFF[c] + n * TILE, TILE)]
        return jnp.dot(mix, block, preferred_element_type=f32)

    def chain_part(buf, c, way, hop):
        at = pl.ds(OFF[c], WIDE[c])
        total = buf.shape[2]
        if hop == NZ // 2:
            return buf.at[way, hop - 1, pl.ds(way * (total // 2), total // 2), at]
        return buf.at[way, hop - 1, :, at]

    def chain_recv(c, way, hop):
        got = got_z if ON_Z[c] else got_y
        arrive(chain_part(got, c, way, hop), c_rs.at[c, way, hop - 1])

    def pass_on(c, hop):
        msg, got = (msg_z, got_z) if ON_Z[c] else (msg_y, got_y)
        half = msg.shape[2] // 2
        for way in (0, 1):
            i = HOP[hop][way]
            if not ON_Z[c] and not (hop == 4 and way == 1):
                returned(c, i)
            if hop < 4:
                chain_recv(c, way, hop + 1)
            side, other = pl.ds(way * half, half), pl.ds((1 - way) * half, half)
            for n in range(WIDE[c] // TILE):
                at = pl.ds(OFF[c] + n * TILE, TILE)
                if hop == 4:
                    msg[way, 3, side, at] = term(c, i, n, side).astype(bf)
                elif hop == 3:
                    came = got[way, 3, side, at].astype(f32)
                    msg[way, 2, side, at] = (term(c, i, n, side) + came).astype(bf)
                    msg[way, 2, other, at] = term(c, i, n, other).astype(bf)
                else:
                    came = got[way, hop, :, at].astype(f32)
                    msg[way, hop - 1, :, at] = (term(c, i, n) + came).astype(bf)
            send(
                chain_part(msg, c, way, hop), chain_part(got, c, way, hop),
                CZ if ON_Z[c] else CY, c_rs.at[c, way, hop - 1], at_z(1 - 2 * way),
            )

    count = jnp.sum(jnp.where(own_span == span_rows, 1.0, 0.0), axis=1, keepdims=True)

    def spread(c):
        mine = everyone.at[d, :, pl.ds(COL[c], WIDE[c])]
        for dx in (1, 3, 2):
            send(mine, mine, X, x_rs.at[c], at_x(dx))
        send(mine, mine, S, s_rs.at[c], sibling)

    def finish_z(c):
        chain_recv(c, 0, 1)
        chain_recv(c, 1, 1)
        for n in range(WIDE[c] // TILE):
            at = pl.ds(OFF[c] + n * TILE, TILE)
            total = term(c, 0, n) + got_z[0, 0, :, at].astype(f32) + got_z[1, 0, :, at].astype(f32)
            fin_out[:, :, at] = total.astype(bf).reshape(NY, spn, TILE)
        at = pl.ds(OFF[c], WIDE[c])
        for j in range(1, NY):
            send(
                fin_out.at[j, :, at], fin_in.at[NY - j, :, at],
                F, f_rs.at[c // 2], at_y(j),
            )

    def finish_z_pooled(c):
        at = pl.ds(OFF[c], WIDE[c])
        total = fin_out[0, :, at].astype(f32)
        arrive(fin_in.at[pl.ds(1, NY - 1), :, at], f_rs.at[c // 2])
        for j in range(1, NY):
            total = total + fin_in[j, :, at].astype(f32)
        everyone[d, :, pl.ds(COL[c], WIDE[c])] = (total / count).astype(bf)
        spread(c)

    def finish_y(c):
        returned(c, 0)
        chain_recv(c, 0, 1)
        chain_recv(c, 1, 1)
        for n in range(WIDE[c] // TILE):
            at = pl.ds(OFF[c] + n * TILE, TILE)
            total = term(c, 0, n) + got_y[0, 0, :, at].astype(f32) + got_y[1, 0, :, at].astype(f32)
            everyone[d, :, pl.ds(COL[c] + n * TILE, TILE)] = (total / count).astype(bf)
        spread(c)

    def relay(c):
        at = pl.ds(COL[c], WIDE[c])
        arrive(everyone.at[pl.ds(0, NX - 1), :, at], x_rs.at[c])
        for dx in (1, 3, 2):
            block = everyone.at[lax.rem(d + 2 * dx, 2 * NX), :, at]
            send(block, block, S, s_rs.at[c], sibling)

    def gathered(c):
        arrive(everyone.at[pl.ds(0, NX), :, pl.ds(COL[c], WIDE[c])], s_rs.at[c])

    band = NY * rows

    def places(c):
        return range(COL[c] // band, (COL[c] + WIDE[c]) // band)

    def bands(c):
        return [BAND[p] for p in places(c)]

    def gradient(c):
        cot_all = cot[...].reshape(groups * spn, columns)
        for p in places(c):
            b = BAND[p]
            lhs = everyone[:, :, pl.ds(p * band, band)].reshape(groups * spn, band)
            out = lax.dot_general(
                lhs, cot_all, (((0,), (0,)), ((), ())), preferred_element_type=f32
            ).astype(bf)
            for q in range(NY):
                part[b, q] = pack(out[q * rows : (q + 1) * rows])
            for j in range(1, NY):
                send(
                    part.at[b, lax.rem(y + j, NY)], part_in.at[b, NY - j],
                    GY, gy_rs.at[b], at_y(j),
                )

    def to_owner(b):
        send(summed.at[b], summed_in.at[z], GZ, gz_rs.at[0], (d, b * NY + y))

    def gather_band(b):
        arrive(part_in.at[b, pl.ds(1, NY - 1)], gy_rs.at[b])
        total = part[b, y].astype(f32)
        for j in range(1, NY):
            total = total + part_in[b, j].astype(f32)

        @pl.when(z == b)
        def _():
            own_sum[...] = total

        @pl.when(z != b)
        def _():
            summed[b] = total.astype(bf)
            to_owner(b)

    def project(c, first=False, final=False):
        def body(n, carry):
            g = pl.ds(2 * n, 2)
            out = lax.dot_general(
                everyone[g, :, pl.ds(COL[c], WIDE[c])].reshape(2 * spn, WIDE[c]),
                w_proj[:, pl.ds(COL[c], WIDE[c])], last, preferred_element_type=f32,
            ).reshape(2, spn, columns)
            if not first:
                out = out + acc[g]
            if final:
                student[g] = out.astype(bf)
            else:
                acc[g] = out
            return carry

        lax.fori_loop(0, groups // 2, body, 0)

    for h in (0, 1):
        select(0, h)
    pl.semaphore_wait(barrier, len(peers))
    for i in range(1, NZ):
        send(meta_out.at[i], meta.at[PAIR[i]], META, meta_rs.at[0], at_z(DELTA[i]))
    for h in (0, 1):
        z_send(tokens, 1, h, 1)
        z_send(tokens, 2, h, -1)
    for h in (0, 1):
        dispatch(0, h)
    arrive(meta.at[pl.ds(1, NZ - 1)], meta_rs.at[0])
    for p in (1, 2, 3):
        a, b = 2 * p - 1, 2 * p
        for h in (0, 1):
            z_recv(a, h)
            if p < 3:
                z_send(zbuf.at[a], a + 2, h, 1)
            elif h == 0:
                z_send(zbuf.at[a], 7, h, 1)
            z_recv(b, h)
            if p < 3:
                z_send(zbuf.at[b], b + 2, h, -1)
            elif h == 1:
                z_send(zbuf.at[b], 7, h, -1)
            dispatch(a, h)
            if p == 1:
                dispatch(b, h)
        if p == 1:
            for j in range(1, NY):
                send(meta, meta_y.at[NY - j], MY, my_rs.at[0], at_y(j))
            for load in loads:
                load.wait()
            ffn(0)
        if p == 2:
            ffn(1)
        if p == 3:
            ffn(2)
    for h in (0, 1):
        z_recv(7, h)
        dispatch(7, h)
    for i in (6, 4):
        for h in (0, 1):
            dispatch(i, h)
    arrive(meta_y.at[pl.ds(1, NY - 1)], my_rs.at[0])
    for i in range(NZ):
        mixing(i)
    for i in (3, 5, 7):
        ffn(i)
    pass_on(ZA, 4)
    pass_on(ZB, 4)
    ffn(6)
    give_back(YA, 5)
    give_back(YA, 7)
    give_back(YA, 6)
    pass_on(ZA, 3)
    pass_on(ZB, 3)
    ffn(4)
    give_back(YA, 3)
    give_back(YA, 4)
    pass_on(ZA, 2)
    give_back(YA, 1)
    give_back(YA, 2)
    give_back(YA, 0)
    pass_on(YA, 4)
    pass_on(ZB, 2)
    give_back(YB, 5)
    give_back(YB, 7)
    give_back(YB, 6)
    pass_on(YA, 3)
    pass_on(ZA, 1)
    give_back(YB, 3)
    give_back(YB, 4)
    pass_on(YA, 2)
    pass_on(ZB, 1)
    give_back(YB, 1)
    give_back(YB, 2)
    give_back(YB, 0)
    pass_on(YA, 1)
    finish_z(ZA)
    finish_y(YA)
    pass_on(YB, 4)
    pass_on(YB, 3)
    finish_z_pooled(ZA)
    finish_z(ZB)
    pass_on(YB, 2)
    relay(YA)
    relay(ZA)
    pass_on(YB, 1)
    gathered(YA)
    gradient(YA)
    finish_z_pooled(ZB)
    finish_y(YB)
    gathered(ZA)
    gradient(ZA)
    for b in bands(YA):
        gather_band(b)
    relay(ZB)
    relay(YB)
    gathered(ZB)
    gradient(ZB)
    gathered(YB)
    gradient(YB)
    for b in bands(ZA):
        gather_band(b)
    project(YA, first=True)
    project(ZA)
    for b in bands(ZB):
        gather_band(b)
    for b in bands(YB):
        gather_band(b)
    project(ZB)
    project(YB, final=True)
    arrive(summed_in.at[pl.ds(0, NZ - 1)], gz_rs.at[0])
    total = own_sum[...]
    for dz in range(1, NZ):
        src = lax.rem(z + dz, NZ)
        total = total + summed_in[src].astype(f32)
    grad[...] = unpack(total, rows)
    sent(meta_out.at[pl.ds(1, NZ - 1)], META)
    sent(meta_y.at[pl.ds(1, NY - 1)], MY)
    sent(zbuf.at[pl.ds(1, NZ - 1)], Z)
    sent(sbuf, Y)
    sent(bbuf.at[:, pl.ds(CAP, (NY - 1) * CAP)], B)
    sent(msg_z.at[:, :, pl.ds(0, 7 * NY * spn // 8)], CZ)
    sent(zbuf.at[pl.ds(0, 7), pl.ds(0, spn), pl.ds(0, Y_WIDE)], CY)
    sent(fin_out.at[pl.ds(1, NY - 1)], F)
    sent(everyone.at[pl.ds(0, NX - 1)], X)
    sent(everyone.at[pl.ds(0, NX)], S)
    sent(part.at[:, pl.ds(1, NY - 1)], GY)
    sent(summed.at[pl.ds(1, NZ - 1)], GZ)


def hand_on(student_in, grad_in, student, grad, sem):
    copies = [
        pltpu.make_async_copy(student_in, student, sem.at[0]),
        pltpu.make_async_copy(grad_in, grad, sem.at[1]),
    ]
    for copy in copies:
        copy.start()
    for copy in copies:
        copy.wait()


def local(tokens, expert_ids, gate_weights, span_ids, w_gate, w_up, w_down, w_proj, cotangent):
    tok, width = tokens.shape
    ff = w_gate.shape[2]
    topk = expert_ids.shape[1]
    spn = tok // 2
    groups, _, columns = cotangent.shape
    rows = width // (NZ * NY)
    packed = (rows * columns // 128, 128)
    bf, f32 = jnp.bfloat16, jnp.float32
    vmem = pl.BlockSpec(memory_space=pltpu.VMEM)
    hbm = pl.BlockSpec(memory_space=pl.ANY)
    scratch, dma = pltpu.VMEM, pltpu.SemaphoreType.DMA
    results = pl.pallas_call(
        kernel,
        out_shape=(
            jax.ShapeDtypeStruct((groups, spn, columns), bf),
            jax.ShapeDtypeStruct((rows, columns), f32),
        ),
        in_specs=[vmem, hbm, vmem, vmem, hbm, hbm, hbm, hbm, hbm],
        out_specs=(vmem, vmem),
        scratch_shapes=[
            scratch((topk, tok), jnp.int32),
            scratch((width, ff), bf),
            scratch((width, ff), bf),
            scratch((ff, width), bf),
            scratch((columns, width), bf),
            scratch((groups, spn, columns), bf),
            scratch((NZ * NY, tok), f32),
            scratch((NZ * NY, tok), f32),
            scratch((NZ, 16, tok), f32),
            scratch((NZ, 16, tok), bf),
            scratch((NZ, 16, tok), bf),
            scratch((NY, NZ, 16, tok), bf),
            scratch((NZ, spn, NY * CAP), bf),
            scratch((NZ, NY * spn, NY * CAP), bf),
            scratch((NZ, tok, width), bf),
            scratch((NZ, (NY - 1) * CAP, width), bf),
            scratch((NZ, NY * CAP, width), bf),
            scratch((NY * CAP, ff), bf),
            scratch((NZ, NY * CAP, width), bf),
            scratch((NZ, NY * CAP, Y_WIDE), bf),
            scratch((2, NZ // 2, spn, Y_WIDE), bf),
            scratch((2, NZ // 2, spn, Y_WIDE), bf),
            scratch((2, NZ // 2, NY * spn, Z_WIDE), bf),
            scratch((2, NZ // 2, NY * spn, Z_WIDE), bf),
            scratch((NY, spn, Z_WIDE), bf),
            scratch((NY, spn, Z_WIDE), bf),
            scratch((groups, spn, width), bf),
            scratch((groups, spn, columns), f32),
            scratch((NZ, NY) + packed, bf),
            scratch((NZ, NY) + packed, bf),
            scratch((NZ,) + packed, bf),
            scratch((NZ,) + packed, bf),
            scratch(packed, f32),
            dma((6,)),
            dma((12,)),
            dma((1,)),
            dma((1,)),
            dma((NZ, 2)),
            dma((NZ,)),
            dma((2, NZ)),
            dma((4, 2, NZ // 2)),
            dma((2,)),
            dma((4,)),
            dma((4,)),
            dma((NZ,)),
            dma((1,)),
        ],
        compiler_params=pltpu.CompilerParams(
            collective_id=0, has_side_effects=True, vmem_limit_bytes=62 * 2**20
        ),
    )(
        tokens, expert_ids.T, gate_weights.T, span_ids, w_gate, w_up, w_down, w_proj.T, cotangent
    )
    return pl.pallas_call(
        hand_on,
        out_shape=[jax.ShapeDtypeStruct(r.shape, r.dtype) for r in results],
        in_specs=[hbm] * 2,
        out_specs=[hbm] * 2,
        scratch_shapes=[dma((2,))],
    )(*results)


def solution(mesh):
    placed = (
        P(("dp", "expert"), None),
        P("dp", None),
        P(("dp", "expert"), None),
        P(None, "expert"),
        P("expert", None, None),
        P("expert", None, None),
        P("expert", None, None),
        P(None, "dp"),
        P(None, "expert", "dp"),
    )
    return jax.shard_map(
        local,
        mesh=mesh,
        in_specs=placed,
        out_specs=(P(None, "expert", "dp"), P("expert", "dp")),
        check_vma=False,
    )
```
